32 devices in a mesh: req: 8 (over z, y), tp: 4 (over x, core).
Axes of the slice: x: 2, y: 2, z: 4, core: 2. Of those that a mesh axis runs over, the one named last changes fastest.
Arguments:
- patches: bfloat16 [2048, 1280], P('req'), may hold values from -6 to 6
- half_grid: int32 [8, 2], P('req'), may hold values from 6 to 8
- text_embed: bfloat16 [1536, 1280], P('req'), may hold values from -6 to 6
- dest_dev: int32 [512], P('req'), may hold values from 0 to 7, as said below
- dest_pos: int32 [512], P('req'), may hold values from 0 to 191, as said below
- text_len: int32 [8], P('req'), may hold values from 1 to 128, as said below
- enc_qkv: bfloat16 [1280, 3840], P('req', 'tp')
- enc_out_t: bfloat16 [1280, 1280], P('req', 'tp'), may hold values from -0.15625 to 0.15625
- enc_up: bfloat16 [1280, 5120], P('req', 'tp'), may hold values from -0.15625 to 0.15625
- enc_down_t: bfloat16 [1280, 5120], P('req', 'tp'), may hold values from -0.078125 to 0.078125
- merge_t: bfloat16 [1280, 5120], P('req', 'tp'), may hold values from -0.078125 to 0.078125
- dec_qkv: bfloat16 [1280, 3840], P('req', 'tp')
- dec_out_t: bfloat16 [1280, 1280], P('req', 'tp'), may hold values from -0.15625 to 0.15625
- dec_up: bfloat16 [1280, 5120], P('req', 'tp'), may hold values from -0.15625 to 0.15625
- dec_down_t: bfloat16 [1280, 5120], P('req', 'tp'), may hold values from -0.078125 to 0.078125
Outputs:
- decoded: bfloat16 [1536, 1280], P('req')
The draws below stay inside these ranges and needn't reach their ends.
Inputs may be any that keep to these rules, and one draw needn't show every extreme that they name: `dest_dev`: the slots of one device go in runs to destination devices; at most 12 slots of one device name one destination device, exactly 12 for some pairs; every device is named by exactly 64 slots in all. `dest_pos`: positions named for one destination device are distinct and below 64 plus its text_len. `text_len`: some request has exactly 128.
All inputs are finite; a program needn't handle non-finite values.
Results may differ from the reference program's by a relative error of at most 0.024.
Values may be sent and summed in bfloat16 or wider, within the bound.
No kernel may reach another device: no remote copies, remote signals or barrier semaphores. Data moves between devices by JAX's collectives and lax.ppermute only.
A program may use at most 64 MiB of HBM per device.

```python
import jax
import jax.numpy as jnp
from jax import lax

D = 1280
HEADS = 16
HEAD_DIM = 80
FF = 5120
GRID = 16
TXT = 128
M_IMG = 64
M_DEV = 64
SEQ = 192
REQS = 8
IMAGES = 8
ENC_TOTAL = 2048
MERGED = 512
DEC_TOTAL = 1536


def qkv_table(key):
    base_table = jax.random.normal(jax.random.fold_in(key, 101), (D, HEADS, 3, HEAD_DIM), jnp.float32) * D ** (-0.5)
    return base_table.reshape(D, HEADS * 3 * HEAD_DIM)


def draw_enc_qkv(key, part):
    return qkv_table(jax.random.fold_in(key, 1)).astype(jnp.bfloat16)


def draw_dec_qkv(key, part):
    return qkv_table(jax.random.fold_in(key, 2)).astype(jnp.bfloat16)


def permute_row(row_key):
    return jax.random.permutation(row_key, SEQ).astype(jnp.int32)


def route_table(key):
    senders = REQS
    slot_count = M_DEV
    even_share = slot_count // senders
    spread_step = max(even_share // 2, 1)
    group_size = senders // 4
    shuffle_order = jax.random.permutation(jax.random.fold_in(key, 201), senders)
    pattern = jnp.full((senders,), even_share, jnp.int32)
    pattern = pattern.at[shuffle_order[:group_size]].add(spread_step)
    pattern = pattern.at[shuffle_order[group_size:2 * group_size]].add(-spread_step)
    run_ends = jnp.cumsum(pattern).astype(jnp.int32)
    run_starts = run_ends - pattern
    slot_ids = jnp.arange(slot_count, dtype=jnp.int32)
    offset = jnp.sum((run_ends[None, :] <= slot_ids[:, None]).astype(jnp.int32), axis=1)
    within = slot_ids - run_starts[offset]
    sender_index = jnp.arange(senders, dtype=jnp.int32)
    target = (sender_index[:, None] + offset[None, :]) % senders
    incoming = pattern[(sender_index[:, None] - sender_index[None, :]) % senders]
    before = jnp.cumsum(incoming, axis=1).astype(jnp.int32) - incoming
    slot_rank = before[target, sender_index[:, None]] + within[None, :]
    text_limit = jax.random.randint(jax.random.fold_in(key, 202), (senders,), 1, TXT + 1)
    fullest = jax.random.randint(jax.random.fold_in(key, 203), (), 0, senders)
    text_limit = jnp.where(sender_index == fullest, TXT, text_limit).astype(jnp.int32)
    length = slot_count + text_limit
    row_keys = jax.random.split(jax.random.fold_in(key, 204), senders)
    shuffled = jax.vmap(permute_row)(row_keys)
    seq_index = jnp.arange(SEQ, dtype=jnp.int32)
    ranking = shuffled + jnp.where(seq_index[None, :] < length[:, None], 0, SEQ).astype(jnp.int32)
    chosen = jnp.sort(jnp.argsort(ranking, axis=1, stable=True)[:, :slot_count].astype(jnp.int32), axis=1)
    position = chosen[target, slot_rank]
    return (target.reshape(-1).astype(jnp.int32), position.reshape(-1).astype(jnp.int32), text_limit)


def draw_dest_dev(key, part):
    return route_table(key)[0]


def draw_dest_pos(key, part):
    return route_table(key)[1]


def draw_text_len(key, part):
    return route_table(key)[2]


def set_ends(entries, stream_key, smallest, top_value):
    longest = entries.shape.index(max(entries.shape))
    spots = []
    for shift in (0, 1):
        where = [jax.random.randint(jax.random.fold_in(stream_key, axis), (), 0, length) for axis, length in enumerate(entries.shape)]
        where[longest] = (where[longest] + shift) % entries.shape[longest]
        spots.append(tuple(where))
    return entries.at[spots[0]].set(smallest).at[spots[1]].set(top_value)


def block_levels(key, extent, cuts, least, high):
    def one(axis_at, shards_of):
        draws = jax.random.uniform(jax.random.fold_in(jax.random.fold_in(key, 6), axis_at), (shards_of,), jnp.float32, least / len(cuts), high / len(cuts))
        return jnp.repeat(jnp.exp(draws), extent[axis_at] // shards_of).reshape((-1,) + (1,) * (len(extent) - axis_at - 1))

    factor_of = one(*cuts[0])
    for cut in cuts[1:]:
        factor_of = factor_of * one(*cut)
    return factor_of


def bell_draw(stream_key, extent, scale, bound, shards=(), held_as=jnp.bfloat16):
    array = jax.random.normal(stream_key, extent, jnp.float32) * scale
    if len(shards) > 0:
        array = block_levels(stream_key, extent, shards, -0.22, 0.18) * array
    return jnp.clip(array, min=-bound, max=bound).astype(held_as)


def setup_inputs(seed: int = 0) -> dict:
    seeds = jax.random.split(jax.random.key(seed), 16)
    return {
        "patches": bell_draw(seeds[0], (ENC_TOTAL, D), 1.0, 6.0, ((0, 8),)),
        "half_grid": set_ends(jax.random.randint(seeds[1], (IMAGES, 2), GRID // 4 + 2, GRID // 2 + 1), jax.random.fold_in(seeds[1], 1), GRID // 4 + 2, (GRID // 2 + 1) - 1).astype(jnp.int32),
        "text_embed": bell_draw(seeds[2], (DEC_TOTAL, D), 1.0, 6.0, ((0, 8),)),
        "dest_dev": draw_dest_dev(jax.random.fold_in(seeds[15], 71), 0),
        "dest_pos": draw_dest_pos(jax.random.fold_in(seeds[15], 71), 0),
        "text_len": draw_text_len(jax.random.fold_in(seeds[15], 71), 0),
        "enc_qkv": draw_enc_qkv(jax.random.fold_in(seeds[15], 71), 0),
        "enc_out_t": bell_draw(seeds[7], (D, D), D ** -0.5, 0.15625, ((0, 8), (1, 4))),
        "enc_up": bell_draw(seeds[8], (D, FF), D ** -0.5, 0.15625, ((0, 8), (1, 4))),
        "enc_down_t": bell_draw(seeds[9], (D, FF), FF ** -0.5, 0.078125, ((0, 8), (1, 4))),
        "merge_t": bell_draw(seeds[10], (D, 4 * D), (4 * D) ** -0.5, 0.078125, ((0, 8), (1, 4))),
        "dec_qkv": draw_dec_qkv(jax.random.fold_in(seeds[15], 71), 0),
        "dec_out_t": bell_draw(seeds[12], (D, D), D ** -0.5, 0.15625, ((0, 8), (1, 4))),
        "dec_up": bell_draw(seeds[13], (D, FF), D ** -0.5, 0.15625, ((0, 8), (1, 4))),
        "dec_down_t": bell_draw(seeds[14], (D, FF), FF ** -0.5, 0.078125, ((0, 8), (1, 4))),
    }


EPS = 1e-06

def normalize(stream):
    values_f = stream.astype(jnp.float32)
    center = values_f - lax.optimization_barrier(jnp.mean(values_f, axis=-1, keepdims=True))
    spread = lax.optimization_barrier(jnp.mean(center * center, axis=-1, keepdims=True))
    return (center * lax.rsqrt(spread + EPS)).astype(jnp.bfloat16)

def attention(normed, w_qkv, w_out_t, allowed):
    length = normed.shape[0]
    projected = jnp.dot(normed, w_qkv, preferred_element_type=jnp.float32).astype(jnp.bfloat16)
    projected = projected.reshape(length, -1, 3, HEAD_DIM).astype(jnp.float32)
    queries = projected[:, :, 0]
    key_part = projected[:, :, 1]
    value_part = projected[:, :, 2]
    scores = jnp.einsum('qhd,khd->hqk', queries, key_part) * HEAD_DIM ** (-0.5)
    scores = jnp.where(allowed[None], scores, -1e+30)
    highest = lax.optimization_barrier(jnp.max(scores, axis=-1, keepdims=True))
    exponent = jnp.exp(scores - highest)
    weights_soft = (exponent / lax.optimization_barrier(jnp.sum(exponent, axis=-1, keepdims=True))).astype(jnp.bfloat16)
    heads_out = jnp.einsum('hqk,khd->qhd', weights_soft.astype(jnp.float32), value_part)
    heads_out = heads_out.astype(jnp.bfloat16).reshape(length, -1)
    return jnp.dot(heads_out, w_out_t.T, preferred_element_type=jnp.float32)

def transformer_layer(stream, weights, allowed):
    w_qkv, w_out_t, w_up, w_down_t = weights
    middle = (stream.astype(jnp.float32) + attention(normalize(stream), w_qkv, w_out_t, allowed)).astype(jnp.bfloat16)
    hidden = jax.nn.gelu(jnp.dot(normalize(middle), w_up, preferred_element_type=jnp.float32), approximate=False)
    hidden = hidden.astype(jnp.bfloat16)
    result_rows = middle.astype(jnp.float32) + jnp.dot(hidden, w_down_t.T, preferred_element_type=jnp.float32)
    return result_rows.astype(jnp.bfloat16)

def reference(patches, half_grid, text_embed, dest_dev, dest_pos, text_len, enc_qkv, enc_out_t, enc_up, enc_down_t, merge_t, dec_qkv, dec_out_t, dec_up, dec_down_t):
    per_image = GRID * GRID
    patch_index = jnp.arange(per_image, dtype=jnp.int32)
    key_valid = ((patch_index // GRID)[None, :] < 2 * half_grid[:, 0:1]) & ((patch_index % GRID)[None, :] < 2 * half_grid[:, 1:2])
    images = patches.reshape(IMAGES, per_image, D)
    enc_weights = (enc_qkv, enc_out_t, enc_up, enc_down_t)

    def run_image(bundle):
        return transformer_layer(bundle[0], enc_weights, bundle[1][None, :])
    encoded = lax.map(run_image, (images, key_valid))
    half_side = GRID // 2
    blocks = encoded.reshape(IMAGES, half_side, 2, half_side, 2, D).transpose(0, 1, 3, 2, 4, 5).reshape(MERGED, 4 * D)
    merged = jnp.dot(blocks, merge_t.T, preferred_element_type=jnp.float32).astype(jnp.bfloat16)
    cell_index = jnp.arange(M_IMG, dtype=jnp.int32)
    slot_valid = ((cell_index // half_side)[None, :] < half_grid[:, 0:1]) & ((cell_index % half_side)[None, :] < half_grid[:, 1:2])
    slot_valid = slot_valid.reshape(MERGED)
    target_pos = jnp.where(slot_valid, dest_pos, SEQ).astype(jnp.int32)
    dec_input = text_embed.reshape(REQS, SEQ, D).at[dest_dev, target_pos].set(merged, mode='drop')
    positions = jnp.arange(SEQ, dtype=jnp.int32)
    causal = positions[:, None] >= positions[None, :]
    dec_weights = (dec_qkv, dec_out_t, dec_up, dec_down_t)

    def run_request(sequence):
        return transformer_layer(sequence, dec_weights, causal)
    decoded = lax.map(run_request, dec_input)
    lengths = M_DEV + text_len
    keep_mask = positions[None, :] < lengths[:, None]
    decoded = jnp.where(keep_mask[:, :, None], decoded, jnp.zeros_like(decoded))
    return decoded.astype(jnp.bfloat16).reshape(DEC_TOTAL, D)
```

```python
import jax
import jax.numpy as jnp
from jax import lax
from jax.sharding import PartitionSpec as P

HEAD_DIM = 80
GRID = 16
HALF = GRID // 2
EPS = 1e-06
AXES = ("req", "tp")


def routes(move):
    groups = lax.axis_size("req") // 8
    pairs = []
    for z in range(4):
        for y in range(2):
            for x in range(2):
                for c in range(2):
                    z2, y2, x2, c2 = move(z, y, x, c)
                    for g in range(groups):
                        source = ((z * 2 + y) * groups + g) * 4 + x * 2 + c
                        target = ((z2 * 2 + y2) * groups + g) * 4 + x2 * 2 + c2
                        pairs.append((source, target))
    return pairs


def swap_core(part):
    return lax.ppermute(part, AXES, routes(lambda z, y, x, c: (z, y, x, 1 - c)))


def swap_x(part):
    return lax.ppermute(part, AXES, routes(lambda z, y, x, c: (z, y, 1 - x, c)))


def swap_y(part):
    return lax.ppermute(part, AXES, routes(lambda z, y, x, c: (z, 1 - y, x, c)))


def swap_z(part, k):
    return lax.ppermute(part, AXES, routes(lambda z, y, x, c: (z ^ k, y, x, c)))


def place():
    index = lax.axis_index("req") // (lax.axis_size("req") // 8)
    tensor = lax.axis_index("tp")
    return index // 2, index % 2, tensor // 2, tensor % 2


def normalize(stream):
    values_f = stream.astype(jnp.float32)
    center = values_f - jnp.mean(values_f, axis=-1, keepdims=True)
    spread = jnp.mean(center * center, axis=-1, keepdims=True)
    return (center * lax.rsqrt(spread + EPS)).astype(jnp.bfloat16)


def to_received_order(rows):
    z, y, _, _ = place()
    width = rows.shape[1] // 8
    return jnp.concatenate(
        [
            lax.dynamic_slice_in_dim(rows, ((z ^ k) * 2 + (y ^ v)) * width, width, 1)
            for v in range(2)
            for k in range(4)
        ],
        axis=1,
    )


def to_plain_order(rows):
    z, y, _, _ = place()
    width = rows.shape[1] // 8
    return jnp.concatenate(
        [
            lax.dynamic_slice_in_dim(rows, ((y ^ b) * 4 + (z ^ a)) * width, width, 1)
            for a in range(4)
            for b in range(2)
        ],
        axis=1,
    )


def from_pair_order(rows):
    lead = rows.shape[:-1]
    width = rows.shape[-1] // 8
    blocks = rows.reshape(lead + (4, 2, width))
    return jnp.concatenate([blocks[..., 1:, :], blocks[..., :1, :]], axis=-2).reshape(rows.shape)


def own_rows(weight):
    groups = lax.axis_size("req") // 8
    if groups == 1:
        return weight
    members = [[i * groups + g for g in range(groups)] for i in range(8)]
    return lax.all_gather(weight, "req", axis=0, tiled=True, axis_index_groups=members)


def gather_blocks(parts):
    column = [parts[0]] + [swap_z(parts[k], k) for k in (1, 2, 3)]
    other_own = swap_y(column[0])
    other_rest = swap_y(jnp.concatenate(column[1:], axis=0))
    return jnp.concatenate(column + [other_own, other_rest], axis=0)


def gather_same(weight):
    return gather_blocks([weight] * 4)


def gather_halved(w_up, w_down_t):
    z, _, _, _ = place()
    half = w_up.shape[1] // 2
    parts = []
    for bit in (0, 1):
        start = ((z % 2) ^ bit) * half
        parts.append(
            jnp.concatenate(
                [
                    lax.dynamic_slice_in_dim(w_up, start, half, 1),
                    lax.dynamic_slice_in_dim(w_down_t, start, half, 1),
                ],
                axis=1,
            )
        )
    both = gather_blocks([parts[0], parts[1], parts[0], parts[1]])
    return both[:, :half], both[:, half:]


def pick(rows, which, axis):
    return lax.dynamic_index_in_dim(rows, which, axis, keepdims=False)


def join_core(half, axis):
    _, _, _, c = place()
    other = swap_core(half)
    first = jnp.where(c == 0, half, other)
    second = jnp.where(c == 0, other, half)
    return jnp.concatenate([first, second], axis=axis)


def add_short(left, right):
    return left.astype(jnp.float32) + right.astype(jnp.float32)


def attention(normed, w_qkv, w_out_t, allowed, split, join):
    total_rows = normed.shape[0]
    projected = jnp.dot(normed, w_qkv, preferred_element_type=jnp.float32).astype(jnp.bfloat16)
    projected = split(projected)
    sample_count, length = projected.shape[:2]
    projected = projected.reshape(sample_count, length, -1, 3, HEAD_DIM)
    queries = projected[:, :, :, 0]
    key_part = projected[:, :, :, 1]
    value_part = projected[:, :, :, 2]
    scores = jnp.einsum(
        "bqhd,bkhd->bhqk", queries, key_part, preferred_element_type=jnp.float32
    ) * HEAD_DIM ** (-0.5)
    scores = jnp.where(allowed, scores, -1e30)
    highest = jnp.max(scores, axis=-1, keepdims=True)
    exponent = jnp.exp(scores - highest)
    weights_soft = (exponent / jnp.sum(exponent, axis=-1, keepdims=True)).astype(jnp.bfloat16)
    heads_out = jnp.einsum(
        "bhqk,bkhd->bqhd", weights_soft, value_part, preferred_element_type=jnp.float32
    )
    heads_out = join(heads_out.astype(jnp.bfloat16).reshape(sample_count, length, -1))
    return lax.dot_general(
        heads_out.reshape(total_rows, -1),
        w_out_t,
        (((1,), (1,)), ((), ())),
        preferred_element_type=jnp.float32,
    )


def middle_half(stream, partial_value):
    _, _, _, c = place()
    rows = stream.shape[0]
    split = partial_value.astype(jnp.bfloat16).reshape(2, rows // 2, -1)
    mine = add_short(pick(split, c, 0), swap_core(pick(split, 1 - c, 0))).astype(jnp.bfloat16)
    total = add_short(mine, swap_x(mine))
    kept = pick(stream.reshape(2, rows // 2, -1), c, 0)
    return (kept.astype(jnp.float32) + total).astype(jnp.bfloat16)


def feed_forward(normed, w_up, w_down_t):
    hidden = jax.nn.gelu(
        jnp.dot(normed, w_up, preferred_element_type=jnp.float32), approximate=False
    ).astype(jnp.bfloat16)
    return lax.dot_general(
        hidden, w_down_t, (((1,), (1,)), ((), ())), preferred_element_type=jnp.float32
    ).astype(jnp.bfloat16)


def paired_feed_forward(mid_half, w_up, w_down_t):
    normed_half = normalize(mid_half)
    pair_half = from_pair_order(swap_z(normed_half, 1))
    own = feed_forward(join_core(normed_half, 0), w_up, w_down_t)
    pair = feed_forward(join_core(pair_half, 0), w_up, w_down_t)
    return own, pair


def sum_pair(own, pair):
    _, _, _, c = place()
    pair_mine = add_short(pick(pair, c, 0), swap_core(pick(pair, 1 - c, 0))).astype(jnp.bfloat16)
    arrived = from_pair_order(swap_z(pair_mine, 1))
    own_mine = add_short(pick(own, c, 0), swap_core(pick(own, 1 - c, 0)))
    return (own_mine + arrived.astype(jnp.float32)).astype(jnp.bfloat16)


def on_device(
    patches,
    half_grid,
    text_embed,
    dest_dev,
    dest_pos,
    text_len,
    enc_qkv,
    enc_out_t,
    enc_up,
    enc_down_t,
    merge_t,
    dec_qkv,
    dec_out_t,
    dec_up,
    dec_down_t,
):
    z, y, x, c = place()
    senders = lax.axis_size("req")
    image_count = half_grid.shape[0]
    model_width = patches.shape[1]
    cells = HALF * HALF
    slot_count = image_count * cells
    qkv_width = enc_qkv.shape[1]

    enc_attn = gather_same(own_rows(jnp.concatenate([enc_qkv, enc_out_t], axis=1)))
    enc_ff = gather_halved(own_rows(enc_up), own_rows(enc_down_t))
    merge_all = gather_same(own_rows(merge_t))
    dec_attn = gather_same(own_rows(jnp.concatenate([dec_qkv, dec_out_t], axis=1)))
    dec_ff = gather_halved(own_rows(dec_up), own_rows(dec_down_t))

    cell_index = jnp.arange(cells, dtype=jnp.int32)
    slot_valid = ((cell_index // HALF)[None, :] < half_grid[:, 0:1]) & (
        (cell_index % HALF)[None, :] < half_grid[:, 1:2]
    )

    rows = patches.reshape(image_count, HALF, 2, HALF, 2, model_width)
    rows = rows.transpose(2, 4, 0, 1, 3, 5).reshape(4 * slot_count, model_width)
    rows = to_received_order(rows)
    key_valid = jnp.tile(slot_valid, (1, 4))

    def by_image(value):
        value = value.reshape(4, image_count, cells, -1).transpose(1, 0, 2, 3)
        return value.reshape(image_count, 4 * cells, -1)

    def by_place(value):
        value = value.reshape(image_count, 4, cells, -1).transpose(1, 0, 2, 3)
        return value.reshape(4 * slot_count, -1)

    def halves(value):
        width = value.shape[1]
        return value.reshape(2, 2, slot_count, width).transpose(1, 0, 2, 3).reshape(-1, width)

    attended = attention(
        normalize(rows),
        enc_attn[:, :qkv_width],
        enc_attn[:, qkv_width:],
        key_valid[:, None, None, :],
        by_image,
        by_place,
    )
    mid_half = middle_half(halves(rows), halves(attended))
    own, pair = paired_feed_forward(mid_half, *enc_ff)
    total = sum_pair(
        own.reshape(2, 2 * slot_count, model_width), pair.reshape(2, 2 * slot_count, model_width)
    ).reshape(2, slot_count, model_width)
    total = add_short(pick(total, x, 0), swap_x(pick(total, 1 - x, 0)))
    kept = pick(mid_half.reshape(2, slot_count, model_width), x, 0)
    encoded = (kept.astype(jnp.float32) + total).astype(jnp.bfloat16)

    partial_merge = lax.dot_general(
        to_plain_order(encoded),
        merge_all,
        (((1,), (1,)), ((), ())),
        preferred_element_type=jnp.float32,
    )
    partial_merge = to_plain_order(partial_merge.astype(jnp.bfloat16))
    half_width = model_width // 2
    partial_merge = partial_merge.reshape(slot_count, 2, half_width)
    merged = add_short(pick(partial_merge, c, 1), swap_core(pick(partial_merge, 1 - c, 1)))
    merged = merged.astype(jnp.bfloat16)
    merged = add_short(merged, swap_x(merged)).astype(jnp.bfloat16)

    even_share = slot_count // senders
    capacity = even_share + max(even_share // 2, 1)
    one_hot = (dest_dev[:, None] == jnp.arange(senders, dtype=jnp.int32)[None, :]).astype(jnp.int32)
    earlier = jnp.cumsum(one_hot, axis=0) - one_hot
    slot_rank = jnp.sum(earlier * one_hot, axis=1)
    bucket = dest_dev * capacity + slot_rank
    chosen = jnp.arange(senders * capacity, dtype=jnp.int32)[:, None] == bucket[None, :]
    digits = jnp.stack([slot_valid.reshape(-1).astype(jnp.int32), dest_pos // 128, dest_pos % 128], 1)
    digits = jnp.pad(digits, ((0, 0), (0, 125))).astype(jnp.bfloat16)
    outgoing = jnp.dot(
        chosen.astype(jnp.bfloat16),
        jnp.concatenate([merged, digits], axis=1),
        preferred_element_type=jnp.float32,
    ).astype(jnp.bfloat16)
    incoming = lax.all_to_all(
        outgoing.reshape(senders, capacity, -1), "req", split_axis=0, concat_axis=0, tiled=True
    ).reshape(senders * capacity, -1)

    seq_len = text_embed.shape[0]
    positions = jnp.arange(seq_len, dtype=jnp.int32)
    marks = incoming[:, half_width:].astype(jnp.int32)
    target = jnp.where(marks[:, 0] > 0, marks[:, 1] * 128 + marks[:, 2], -1)
    hits = positions[:, None] == target[None, :]
    placed = jnp.dot(
        hits.astype(jnp.bfloat16), incoming[:, :half_width], preferred_element_type=jnp.float32
    ).astype(jnp.bfloat16)
    text_half = lax.dynamic_slice_in_dim(text_embed, c * half_width, half_width, 1)
    dec_half = jnp.where(jnp.any(hits, axis=1)[:, None], placed, text_half)
    dec_rows = to_received_order(join_core(dec_half, 1))

    causal = (positions[:, None] >= positions[None, :])[None, None]
    attended = attention(
        normalize(dec_rows),
        dec_attn[:, :qkv_width],
        dec_attn[:, qkv_width:],
        causal,
        lambda value: value[None],
        lambda value: value[0],
    )
    mid_half = middle_half(dec_rows, attended)
    own, pair = paired_feed_forward(mid_half, *dec_ff)
    half_rows = seq_len // 2
    total = sum_pair(
        own.reshape(2, half_rows, model_width), pair.reshape(2, half_rows, model_width)
    )
    total = add_short(total, swap_x(total))
    decoded = (mid_half.astype(jnp.float32) + total).astype(jnp.bfloat16)
    keep_mask = positions < slot_count + text_len[0]
    keep_half = pick(keep_mask.reshape(2, half_rows), c, 0)
    decoded = jnp.where(keep_half[:, None], decoded, jnp.zeros_like(decoded))
    return join_core(to_plain_order(decoded), 0)


def solution(mesh):
    return jax.shard_map(
        on_device,
        mesh=mesh,
        in_specs=(
            P("req", None),
            P("req", None),
            P("req", None),
            P("req"),
            P("req"),
            P("req"),
            P("req", "tp"),
            P("req", "tp"),
            P("req", "tp"),
            P("req", "tp"),
            P("req", "tp"),
            P("req", "tp"),
            P("req", "tp"),
            P("req", "tp"),
            P("req", "tp"),
        ),
        out_specs=P("req", None),
        check_vma=False,
    )
```

```python
import jax
import jax.numpy as jnp
from jax import lax
from jax.sharding import PartitionSpec as P

HEAD_DIM = 80
GRID = 16
HALF = GRID // 2
EPS = 1e-06
AXES = ("req", "tp")


def routes(move):
    groups = lax.axis_size("req") // 8
    pairs = []
    for z in range(4):
        for y in range(2):
            for x in range(2):
                for c in range(2):
                    z2, y2, x2, c2 = move(z, y, x, c)
                    for g in range(groups):
                        source = ((z * 2 + y) * groups + g) * 4 + x * 2 + c
                        target = ((z2 * 2 + y2) * groups + g) * 4 + x2 * 2 + c2
                        pairs.append((source, target))
    return pairs


def swap_core(part):
    return lax.ppermute(part, AXES, routes(lambda z, y, x, c: (z, y, x, 1 - c)))


def swap_x(part):
    return lax.ppermute(part, AXES, routes(lambda z, y, x, c: (z, y, 1 - x, c)))


def swap_y(part):
    return lax.ppermute(part, AXES, routes(lambda z, y, x, c: (z, 1 - y, x, c)))


def swap_z(part, k):
    return lax.ppermute(part, AXES, routes(lambda z, y, x, c: (z ^ k, y, x, c)))


def place():
    index = lax.axis_index("req") // (lax.axis_size("req") // 8)
    tensor = lax.axis_index("tp")
    return index // 2, index % 2, tensor // 2, tensor % 2


def normalize(stream):
    values_f = stream.astype(jnp.float32)
    center = values_f - jnp.mean(values_f, axis=-1, keepdims=True)
    spread = jnp.mean(center * center, axis=-1, keepdims=True)
    return (center * lax.rsqrt(spread + EPS)).astype(jnp.bfloat16)


def to_received_order(rows):
    z, y, _, _ = place()
    width = rows.shape[1] // 8
    return jnp.concatenate(
        [
            lax.dynamic_slice_in_dim(rows, ((z ^ k) * 2 + (y ^ v)) * width, width, 1)
            for v in range(2)
            for k in range(4)
        ],
        axis=1,
    )


def to_plain_order(rows):
    z, y, _, _ = place()
    width = rows.shape[1] // 8
    return jnp.concatenate(
        [
            lax.dynamic_slice_in_dim(rows, ((y ^ b) * 4 + (z ^ a)) * width, width, 1)
            for a in range(4)
            for b in range(2)
        ],
        axis=1,
    )


def from_pair_order(rows):
    lead = rows.shape[:-1]
    width = rows.shape[-1] // 8
    blocks = rows.reshape(lead + (4, 2, width))
    return jnp.concatenate([blocks[..., 1:, :], blocks[..., :1, :]], axis=-2).reshape(rows.shape)


def own_rows(weight):
    groups = lax.axis_size("req") // 8
    if groups == 1:
        return weight
    members = [[i * groups + g for g in range(groups)] for i in range(8)]
    return lax.all_gather(weight, "req", axis=0, tiled=True, axis_index_groups=members)


def together(*values):
    return lax.optimization_barrier(values)


class Same:
    def __init__(self, weight):
        self.own = weight
        self.first = swap_z(weight, 1)
        self.second = swap_z(weight, 2)
        self.y_own = swap_y(weight)

    def forward(self):
        self.third = swap_z(self.second, 1)
        self.y_early = swap_y(jnp.concatenate([self.first, self.second], axis=0))

    def finish(self):
        y_third = swap_y(self.third)
        return jnp.concatenate(
            [self.own, self.first, self.second, self.third, self.y_own, self.y_early, y_third], axis=0
        )


class Halved:
    def __init__(self, w_up, w_down_t):
        z, _, _, _ = place()
        half = w_up.shape[1] // 2
        parts = []
        for bit in (0, 1):
            start = ((z % 2) ^ bit) * half
            parts.append(
                jnp.concatenate(
                    [
                        lax.dynamic_slice_in_dim(w_up, start, half, 1),
                        lax.dynamic_slice_in_dim(w_down_t, start, half, 1),
                    ],
                    axis=1,
                )
            )
        self.half = half
        self.own = parts[0]
        self.first = swap_z(parts[1], 1)
        self.second = swap_z(parts[0], 2)
        self.third = swap_z(parts[1], 3)
        self.y_own = swap_y(parts[0])

    def forward(self):
        self.y_early = swap_y(jnp.concatenate([self.first, self.second], axis=0))

    def finish(self):
        y_third = swap_y(self.third)
        both = jnp.concatenate(
            [self.own, self.first, self.second, self.third, self.y_own, self.y_early, y_third], axis=0
        )
        return both[:, : self.half], both[:, self.half :]


def pick(rows, which, axis):
    return lax.dynamic_index_in_dim(rows, which, axis, keepdims=False)


def join_core(half, axis):
    _, _, _, c = place()
    other = swap_core(half)
    first = jnp.where(c == 0, half, other)
    second = jnp.where(c == 0, other, half)
    return jnp.concatenate([first, second], axis=axis)


def add_short(left, right):
    return left.astype(jnp.float32) + right.astype(jnp.float32)


def attention(normed, w_qkv, w_out_t, allowed, split, join):
    total_rows = normed.shape[0]
    projected = jnp.dot(normed, w_qkv, preferred_element_type=jnp.float32).astype(jnp.bfloat16)
    projected = split(projected)
    sample_count, length = projected.shape[:2]
    projected = projected.reshape(sample_count, length, -1, 3, HEAD_DIM)
    queries = projected[:, :, :, 0]
    key_part = projected[:, :, :, 1]
    value_part = projected[:, :, :, 2]
    scores = jnp.einsum(
        "bqhd,bkhd->bhqk", queries, key_part, preferred_element_type=jnp.float32
    ) * HEAD_DIM ** (-0.5)
    scores = jnp.where(allowed, scores, -1e30)
    highest = jnp.max(scores, axis=-1, keepdims=True)
    exponent = jnp.exp(scores - highest)
    weights_soft = (exponent / jnp.sum(exponent, axis=-1, keepdims=True)).astype(jnp.bfloat16)
    heads_out = jnp.einsum(
        "bhqk,bkhd->bqhd", weights_soft, value_part, preferred_element_type=jnp.float32
    )
    heads_out = join(heads_out.astype(jnp.bfloat16).reshape(sample_count, length, -1))
    return lax.dot_general(
        heads_out.reshape(total_rows, -1),
        w_out_t,
        (((1,), (1,)), ((), ())),
        preferred_element_type=jnp.float32,
    )


def middle_half(stream, partial_value):
    _, _, _, c = place()
    rows = stream.shape[0]
    split = partial_value.astype(jnp.bfloat16).reshape(2, rows // 2, -1)
    mine = add_short(pick(split, c, 0), swap_core(pick(split, 1 - c, 0))).astype(jnp.bfloat16)
    total = add_short(mine, swap_x(mine))
    kept = pick(stream.reshape(2, rows // 2, -1), c, 0)
    return (kept.astype(jnp.float32) + total).astype(jnp.bfloat16)


def feed_forward(normed, w_up, w_down_t):
    hidden = jax.nn.gelu(
        jnp.dot(normed, w_up, preferred_element_type=jnp.float32), approximate=False
    ).astype(jnp.bfloat16)
    return lax.dot_general(
        hidden, w_down_t, (((1,), (1,)), ((), ())), preferred_element_type=jnp.float32
    ).astype(jnp.bfloat16)


def sum_core(values):
    _, _, _, c = place()
    return add_short(pick(values, c, 0), swap_core(pick(values, 1 - c, 0)))


def exchange_blocks(blocks):
    z, y, _, _ = place()
    groups = blocks.shape[1]
    if groups > 1:
        members = [[i * groups + g for g in range(groups)] for i in range(8)]
        blocks = lax.all_to_all(
            blocks, "req", split_axis=1, concat_axis=1, tiled=True, axis_index_groups=members
        )
    blocks = blocks.reshape((4, 2) + blocks.shape[1:])
    kept = pick(blocks, y, 1)
    other = swap_y(pick(blocks, 1 - y, 1))
    both = jnp.stack([kept, other], axis=1)
    mixed = [pick(both, z, 0)] + [swap_z(pick(both, z ^ k, 0), k) for k in (1, 2, 3)]
    return jnp.concatenate(mixed, axis=0)


def on_device(
    patches,
    half_grid,
    text_embed,
    dest_dev,
    dest_pos,
    text_len,
    enc_qkv,
    enc_out_t,
    enc_up,
    enc_down_t,
    merge_t,
    dec_qkv,
    dec_out_t,
    dec_up,
    dec_down_t,
):
    z, y, x, c = place()
    senders = lax.axis_size("req")
    image_count = half_grid.shape[0]
    model_width = patches.shape[1]
    cells = HALF * HALF
    slot_count = image_count * cells
    qkv_width = enc_qkv.shape[1]

    enc_attn = Same(own_rows(jnp.concatenate([enc_qkv, enc_out_t], axis=1)))
    enc_up, enc_down_t = own_rows(enc_up), own_rows(enc_down_t)
    merge_t = own_rows(merge_t)
    dec_attn = own_rows(jnp.concatenate([dec_qkv, dec_out_t], axis=1))
    dec_up, dec_down_t = own_rows(dec_up), own_rows(dec_down_t)

    enc_attn.second, enc_up, enc_down_t = together(enc_attn.second, enc_up, enc_down_t)
    enc_attn.forward()
    enc_ff = Halved(enc_up, enc_down_t)
    w_enc_attn = enc_attn.finish()

    cell_index = jnp.arange(cells, dtype=jnp.int32)
    slot_valid = ((cell_index // HALF)[None, :] < half_grid[:, 0:1]) & (
        (cell_index % HALF)[None, :] < half_grid[:, 1:2]
    )

    rows = patches.reshape(image_count, HALF, 2, HALF, 2, model_width)
    rows = rows.transpose(2, 4, 0, 1, 3, 5).reshape(4 * slot_count, model_width)
    rows = to_received_order(rows)
    key_valid = jnp.tile(slot_valid, (1, 4))

    def by_image(value):
        value = value.reshape(4, image_count, cells, -1).transpose(1, 0, 2, 3)
        return value.reshape(image_count, 4 * cells, -1)

    def by_place(value):
        value = value.reshape(image_count, 4, cells, -1).transpose(1, 0, 2, 3)
        return value.reshape(4 * slot_count, -1)

    def halves(value):
        width = value.shape[1]
        return value.reshape(2, 2, slot_count, width).transpose(1, 0, 2, 3).reshape(-1, width)

    attended = attention(
        normalize(rows),
        w_enc_attn[:, :qkv_width],
        w_enc_attn[:, qkv_width:],
        key_valid[:, None, None, :],
        by_image,
        by_place,
    )
    mid_half = middle_half(halves(rows), halves(attended))
    normed_half = normalize(mid_half)
    normed_half, enc_ff.first, enc_ff.second, enc_ff.third, merge_t = together(
        normed_half, enc_ff.first, enc_ff.second, enc_ff.third, merge_t
    )
    pair_half = swap_z(normed_half, 1)
    enc_ff.forward()
    w_enc_ff = enc_ff.finish()
    merge_all = Same(merge_t)
    own = feed_forward(join_core(normed_half, 0), *w_enc_ff)
    pair_rows = join_core(from_pair_order(pair_half), 0)
    pair_rows, merge_all.first, merge_all.second = together(
        pair_rows, merge_all.first, merge_all.second
    )
    merge_all.forward()
    pair = feed_forward(pair_rows, *w_enc_ff)
    pair = pair.reshape(2, 2 * slot_count, model_width)
    pair_mine = sum_core(pair).astype(jnp.bfloat16)
    pair_mine, dec_attn = together(pair_mine, dec_attn)
    arrived = swap_z(pair_mine, 1)
    dec_attn = Same(dec_attn)
    own_mine = sum_core(own.reshape(2, 2 * slot_count, model_width))
    arrived, merge_all.third = together(arrived, merge_all.third)
    w_merge = merge_all.finish()
    total = own_mine + from_pair_order(arrived).astype(jnp.float32)
    total = total.astype(jnp.bfloat16).reshape(2, slot_count, model_width)
    total = add_short(pick(total, x, 0), swap_x(pick(total, 1 - x, 0)))
    kept = pick(mid_half.reshape(2, slot_count, model_width), x, 0)
    encoded = (kept.astype(jnp.float32) + total).astype(jnp.bfloat16)

    encoded, dec_attn.first, dec_attn.second = together(
        encoded, dec_attn.first, dec_attn.second
    )
    dec_attn.forward()
    partial_merge = lax.dot_general(
        to_plain_order(encoded),
        w_merge,
        (((1,), (1,)), ((), ())),
        preferred_element_type=jnp.float32,
    )
    partial_merge = to_plain_order(partial_merge.astype(jnp.bfloat16))
    half_width = model_width // 2
    partial_merge = partial_merge.reshape(slot_count, 2, half_width)
    merged = add_short(pick(partial_merge, c, 1), swap_core(pick(partial_merge, 1 - c, 1)))
    merged = merged.astype(jnp.bfloat16)
    merged = add_short(merged, swap_x(merged)).astype(jnp.bfloat16)

    even_share = slot_count // senders
    capacity = even_share + max(even_share // 2, 1)
    one_hot = (dest_dev[:, None] == jnp.arange(senders, dtype=jnp.int32)[None, :]).astype(jnp.int32)
    earlier = jnp.cumsum(one_hot, axis=0) - one_hot
    slot_rank = jnp.sum(earlier * one_hot, axis=1)
    bucket = dest_dev * capacity + slot_rank
    chosen = jnp.arange(senders * capacity, dtype=jnp.int32)[:, None] == bucket[None, :]
    digits = jnp.stack([slot_valid.reshape(-1).astype(jnp.int32), dest_pos // 128, dest_pos % 128], 1)
    digits = jnp.pad(digits, ((0, 0), (0, 125))).astype(jnp.bfloat16)
    outgoing = jnp.dot(
        chosen.astype(jnp.bfloat16),
        jnp.concatenate([merged, digits], axis=1),
        preferred_element_type=jnp.float32,
    ).astype(jnp.bfloat16)
    outgoing, dec_up, dec_down_t = together(outgoing, dec_up, dec_down_t)
    incoming = exchange_blocks(outgoing.reshape(8, senders // 8, capacity, -1))
    dec_ff = Halved(dec_up, dec_down_t)
    incoming, dec_attn.third = together(incoming, dec_attn.third)
    w_dec_attn = dec_attn.finish()
    incoming = incoming.reshape(senders * capacity, -1)

    seq_len = text_embed.shape[0]
    positions = jnp.arange(seq_len, dtype=jnp.int32)
    marks = incoming[:, half_width:].astype(jnp.int32)
    target = jnp.where(marks[:, 0] > 0, marks[:, 1] * 128 + marks[:, 2], -1)
    hits = positions[:, None] == target[None, :]
    placed = jnp.dot(
        hits.astype(jnp.bfloat16), incoming[:, :half_width], preferred_element_type=jnp.float32
    ).astype(jnp.bfloat16)
    text_half = lax.dynamic_slice_in_dim(text_embed, c * half_width, half_width, 1)
    dec_half = jnp.where(jnp.any(hits, axis=1)[:, None], placed, text_half)
    dec_rows = to_received_order(join_core(dec_half, 1))

    causal = (positions[:, None] >= positions[None, :])[None, None]
    attended = attention(
        normalize(dec_rows),
        w_dec_attn[:, :qkv_width],
        w_dec_attn[:, qkv_width:],
        causal,
        lambda value: value[None],
        lambda value: value[0],
    )
    mid_half = middle_half(dec_rows, attended)
    normed_half = normalize(mid_half)
    normed_half, dec_ff.first, dec_ff.second, dec_ff.third = together(
        normed_half, dec_ff.first, dec_ff.second, dec_ff.third
    )
    pair_half = swap_z(normed_half, 1)
    dec_ff.forward()
    w_dec_ff = dec_ff.finish()
    half_rows = seq_len // 2
    own = feed_forward(join_core(normed_half, 0), *w_dec_ff)
    pair = feed_forward(join_core(from_pair_order(pair_half), 0), *w_dec_ff)
    pair_mine = sum_core(pair.reshape(2, half_rows, model_width)).astype(jnp.bfloat16)
    arrived = swap_z(pair_mine, 1)
    own_mine = sum_core(own.reshape(2, half_rows, model_width))
    total = (own_mine + from_pair_order(arrived).astype(jnp.float32)).astype(jnp.bfloat16)
    total = add_short(total, swap_x(total))
    decoded = (mid_half.astype(jnp.float32) + total).astype(jnp.bfloat16)
    keep_mask = positions < slot_count + text_len[0]
    keep_half = pick(keep_mask.reshape(2, half_rows), c, 0)
    decoded = jnp.where(keep_half[:, None], decoded, jnp.zeros_like(decoded))
    return join_core(to_plain_order(decoded), 0)


def solution(mesh):
    return jax.shard_map(
        on_device,
        mesh=mesh,
        in_specs=(
            P("req", None),
            P("req", None),
            P("req", None),
            P("req"),
            P("req"),
            P("req"),
            P("req", "tp"),
            P("req", "tp"),
            P("req", "tp"),
            P("req", "tp"),
            P("req", "tp"),
            P("req", "tp"),
            P("req", "tp"),
            P("req", "tp"),
            P("req", "tp"),
        ),
        out_specs=P("req", None),
        check_vma=False,
    )
```

```python
import jax
import jax.numpy as jnp
from jax import lax
from jax.experimental import pallas as pl
from jax.experimental.pallas import tpu as pltpu
from jax.sharding import PartitionSpec as P

HEAD_DIM = 80
GRID = 16
HALF = GRID // 2
EPS = 1e-06
AXES = ("req", "tp")


def routes(move):
    groups = lax.axis_size("req") // 8
    pairs = []
    for z in range(4):
        for y in range(2):
            for x in range(2):
                for c in range(2):
                    z2, y2, x2, c2 = move(z, y, x, c)
                    for g in range(groups):
                        source = ((z * 2 + y) * groups + g) * 4 + x * 2 + c
                        target = ((z2 * 2 + y2) * groups + g) * 4 + x2 * 2 + c2
                        pairs.append((source, target))
    return pairs


def swap_core(part):
    return lax.ppermute(part, AXES, routes(lambda z, y, x, c: (z, y, x, 1 - c)))


def swap_x(part):
    return lax.ppermute(part, AXES, routes(lambda z, y, x, c: (z, y, 1 - x, c)))


def swap_y(part):
    return lax.ppermute(part, AXES, routes(lambda z, y, x, c: (z, 1 - y, x, c)))


def swap_z(part, k):
    return lax.ppermute(part, AXES, routes(lambda z, y, x, c: (z ^ k, y, x, c)))


def place():
    index = lax.axis_index("req") // (lax.axis_size("req") // 8)
    tensor = lax.axis_index("tp")
    return index // 2, index % 2, tensor // 2, tensor % 2


def own_rows(weight):
    groups = lax.axis_size("req") // 8
    if groups == 1:
        return weight
    members = [[i * groups + g for g in range(groups)] for i in range(8)]
    return lax.all_gather(weight, "req", axis=0, tiled=True, axis_index_groups=members)


def all_rows(weight):
    return lax.all_gather(weight, "req", axis=0, tiled=True)


def together(*values):
    return lax.optimization_barrier(values)


class Same:
    def __init__(self, weight):
        self.own = weight
        self.first = swap_z(weight, 1)
        self.second = swap_z(weight, 2)
        self.y_own = swap_y(weight)

    def forward(self):
        self.third = swap_z(self.second, 1)
        self.y_early = swap_y(jnp.concatenate([self.first, self.second], axis=0))

    def pieces(self):
        y_third = swap_y(self.third)
        return [self.own, self.first, self.second, self.third, self.y_own, self.y_early, y_third]


class Halved:
    def __init__(self, w_up, w_down_t):
        z, _, _, _ = place()
        half = w_up.shape[1] // 2
        parts = []
        for bit in (0, 1):
            start = ((z % 2) ^ bit) * half
            parts.append(
                jnp.concatenate(
                    [
                        lax.dynamic_slice_in_dim(w_up, start, half, 1),
                        lax.dynamic_slice_in_dim(w_down_t, start, half, 1),
                    ],
                    axis=1,
                )
            )
        self.own = parts[0]
        self.first = swap_z(parts[1], 1)
        self.second = swap_z(parts[0], 2)
        self.third = swap_z(parts[1], 3)
        self.y_own = swap_y(parts[0])

    def forward(self):
        self.y_early = swap_y(jnp.concatenate([self.first, self.second], axis=0))

    def pieces(self):
        y_third = swap_y(self.third)
        return [self.own, self.first, self.second, self.third, self.y_own, self.y_early, y_third]


def block_places():
    z, y, _, c = place()
    spots = [(z ^ k) * 2 + (y ^ v) for v in range(2) for k in range(4)]
    return jnp.stack(spots + [c]).astype(jnp.int32)


def load_weight(spots, pieces, weight, sems):
    if len(pieces) == 1:
        copies = [pltpu.make_async_copy(pieces[0], weight, sems.at[0])]
    else:
        height = weight.shape[0] // 8
        copies = []
        for piece in pieces:
            for block in range(piece.shape[0] // height):
                at = len(copies)
                start = pl.multiple_of(spots[at] * height, 16)
                copies.append(
                    pltpu.make_async_copy(
                        piece.at[pl.ds(block * height, height)],
                        weight.at[pl.ds(start, height)],
                        sems.at[at],
                    )
                )
    for copy in copies:
        copy.start()
    return copies


def norm(values_f):
    center = values_f - jnp.mean(values_f, axis=-1, keepdims=True)
    spread = jnp.mean(center * center, axis=-1, keepdims=True)
    return (center * lax.rsqrt(spread + EPS)).astype(jnp.bfloat16)


def dot_t(left, right):
    return lax.dot_general(left, right, (((1,), (1,)), ((), ())), preferred_element_type=jnp.float32)


VMEM = pl.BlockSpec(memory_space=pltpu.VMEM)
SMEM = pl.BlockSpec(memory_space=pltpu.SMEM)
ANY = pl.BlockSpec(memory_space=pl.ANY)


def local_call(kernel, ins, in_specs, outs, scratch):
    return pl.pallas_call(
        kernel,
        in_specs=in_specs,
        out_specs=[VMEM] * len(outs),
        out_shape=[jax.ShapeDtypeStruct(shape, jnp.bfloat16) for shape in outs],
        scratch_shapes=scratch,
        cost_estimate=pl.CostEstimate(flops=0, bytes_accessed=0, transcendentals=0),
        compiler_params=pltpu.CompilerParams(vmem_limit_bytes=32 * 2**20),
    )(*ins)


def attention(spots, rows, allowed, pieces, qkv_width):
    length, width = rows.shape
    heads = qkv_width // (3 * HEAD_DIM)
    half = length // 2

    def kernel(spots_ref, rows_ref, allowed_ref, *refs):
        piece_refs = refs[: len(pieces)]
        keep, send, weight, projected, mixed, sems = refs[len(pieces) :]
        copies = load_weight(spots_ref, piece_refs, weight, sems)
        normed = norm(rows_ref[...].astype(jnp.float32))
        mixed[...] = jnp.zeros_like(mixed)
        for copy in copies:
            copy.wait()
        projected[...] = (
            jnp.dot(normed, weight[...], preferred_element_type=jnp.float32)
            .astype(jnp.bfloat16)
            .astype(jnp.float32)
        )
        for head in range(heads):
            at = head * 3 * HEAD_DIM
            query = projected[:, at : at + HEAD_DIM].astype(jnp.bfloat16)
            key = projected[:, at + HEAD_DIM : at + 2 * HEAD_DIM].astype(jnp.bfloat16)
            value = projected[:, at + 2 * HEAD_DIM : at + 3 * HEAD_DIM].astype(jnp.bfloat16)
            scores = dot_t(query, key) * HEAD_DIM ** (-0.5)
            scores = jnp.where(allowed_ref[...] > 0, scores, -1e30)
            exponent = jnp.exp(scores - jnp.max(scores, axis=-1, keepdims=True))
            soft = (exponent / jnp.sum(exponent, axis=-1, keepdims=True)).astype(jnp.bfloat16)
            out_at = qkv_width + head * HEAD_DIM
            mixed[:, out_at : out_at + HEAD_DIM] = jnp.dot(
                soft, value, preferred_element_type=jnp.float32
            )
        projected[...] = dot_t(mixed[...].astype(jnp.bfloat16), weight[...])
        core = spots_ref[8]
        keep[...] = projected[pl.ds(pl.multiple_of(core * half, 16), half), :].astype(jnp.bfloat16)
        send[...] = projected[pl.ds(pl.multiple_of((1 - core) * half, 16), half), :].astype(
            jnp.bfloat16
        )

    return local_call(
        kernel,
        [spots, rows, allowed] + pieces,
        [SMEM, VMEM, VMEM] + [ANY] * len(pieces),
        [(half, width)] * 2,
        [
            pltpu.VMEM((width, width), jnp.bfloat16),
            pltpu.VMEM((length, width), jnp.float32),
            pltpu.VMEM((length, width), jnp.float32),
            pltpu.SemaphoreType.DMA((8,)),
        ],
    )


def middle(spots, rows, left, right):
    half, width = left.shape

    def kernel(spots_ref, rows_ref, left_ref, right_ref, mid, normed):
        base = rows_ref[pl.ds(pl.multiple_of(spots_ref[8] * half, 16), half), :]
        total = left_ref[...].astype(jnp.float32) + right_ref[...].astype(jnp.float32)
        value = (base.astype(jnp.float32) + total).astype(jnp.bfloat16)
        mid[...] = value
        normed[...] = norm(value.astype(jnp.float32))

    return local_call(
        kernel, [spots, rows, left, right], [SMEM, VMEM, VMEM, VMEM], [(half, width)] * 2, []
    )


def feed_forward(spots, mine, others, pieces):
    half, width = mine.shape
    units = width // 2

    def kernel(spots_ref, mine_ref, others_ref, *refs):
        piece_refs = refs[: len(pieces)]
        keep, send, weight, sems = refs[len(pieces) :]
        for copy in load_weight(spots_ref, piece_refs, weight, sems):
            copy.wait()
        for source, target in ((others_ref, send), (mine_ref, keep)):
            hidden = jnp.dot(
                source[...], weight[:, :units], preferred_element_type=jnp.float32
            )
            hidden = 0.5 * hidden * (1.0 + lax.erf(hidden * 0.5**0.5))
            target[...] = dot_t(hidden.astype(jnp.bfloat16), weight[:, units:]).astype(jnp.bfloat16)

    return local_call(
        kernel,
        [spots, mine, others] + pieces,
        [SMEM, VMEM, VMEM] + [ANY] * len(pieces),
        [(half, width)] * 2,
        [pltpu.VMEM((width, width), jnp.bfloat16), pltpu.SemaphoreType.DMA((8,))],
    )


def pick(rows, which, axis):
    return lax.dynamic_index_in_dim(rows, which, axis, keepdims=False)


def add_short(left, right):
    return left.astype(jnp.float32) + right.astype(jnp.float32)


def join_core(half, axis):
    _, _, _, c = place()
    other = swap_core(half)
    first = jnp.where(c == 0, half, other)
    second = jnp.where(c == 0, other, half)
    return jnp.concatenate([first, second], axis=axis)


def exchange_blocks(blocks):
    z, y, _, _ = place()
    groups = blocks.shape[1]
    if groups > 1:
        members = [[i * groups + g for g in range(groups)] for i in range(8)]
        blocks = lax.all_to_all(
            blocks, "req", split_axis=1, concat_axis=1, tiled=True, axis_index_groups=members
        )
    blocks = blocks.reshape((4, 2) + blocks.shape[1:])
    kept = pick(blocks, y, 1)
    other = swap_y(pick(blocks, 1 - y, 1))
    both = jnp.stack([kept, other], axis=1)
    mixed = [pick(both, z, 0)] + [swap_z(pick(both, z ^ k, 0), k) for k in (1, 2, 3)]
    return jnp.concatenate(mixed, axis=0)


def on_device(
    patches,
    half_grid,
    text_embed,
    dest_dev,
    dest_pos,
    text_len,
    enc_qkv,
    enc_out_t,
    enc_up,
    enc_down_t,
    merge_t,
    dec_qkv,
    dec_out_t,
    dec_up,
    dec_down_t,
):
    _, _, x, c = place()
    senders = lax.axis_size("req")
    image_count = half_grid.shape[0]
    model_width = patches.shape[1]
    cells = HALF * HALF
    slot_count = image_count * cells
    qkv_width = enc_qkv.shape[1]
    half_width = model_width // 2
    spots = block_places()

    enc_attn = Same(own_rows(jnp.concatenate([enc_qkv, enc_out_t], axis=1)))
    enc_up, enc_down_t = own_rows(enc_up), own_rows(enc_down_t)
    dec_up, dec_down_t = own_rows(dec_up), own_rows(dec_down_t)
    enc_attn.second, enc_up, enc_down_t = together(enc_attn.second, enc_up, enc_down_t)
    enc_attn.forward()
    enc_ff = Halved(enc_up, enc_down_t)
    enc_attn_pieces = enc_attn.pieces()

    cell_index = jnp.arange(cells, dtype=jnp.int32)
    slot_valid = ((cell_index // HALF)[None, :] < half_grid[:, 0:1]) & (
        (cell_index % HALF)[None, :] < half_grid[:, 1:2]
    )
    slot_valid = slot_valid.reshape(-1)

    rows = patches.reshape(image_count, HALF, 2, HALF, 2, model_width)
    rows = rows.transpose(4, 2, 0, 1, 3, 5).reshape(4 * slot_count, model_width)
    image_of = jnp.tile(jnp.arange(slot_count, dtype=jnp.int32) // cells, 4)
    allowed = (image_of[:, None] == image_of[None, :]) & jnp.tile(slot_valid, 4)[None, :]
    allowed = allowed.astype(jnp.float32)

    rows, enc_ff.first, merge_t, dec_qkv, dec_out_t = together(
        rows, enc_ff.first, merge_t, dec_qkv, dec_out_t
    )
    w_merge = all_rows(merge_t)
    w_dec_attn = all_rows(jnp.concatenate([dec_qkv, dec_out_t], axis=1))
    keep, send = attention(spots, rows, allowed, enc_attn_pieces, qkv_width)
    mine = add_short(keep, swap_core(send)).astype(jnp.bfloat16)
    mine, enc_ff.second = together(mine, enc_ff.second)
    enc_ff.forward()
    mid, normed = middle(spots, rows, mine, swap_x(mine))
    normed, enc_ff.third = together(normed, enc_ff.third)
    enc_ff_pieces = enc_ff.pieces()
    normed_pair = swap_z(normed, 1)
    own_keep, own_send = feed_forward(spots, normed, swap_core(normed), enc_ff_pieces)
    pair_keep, pair_send = feed_forward(spots, normed_pair, swap_core(normed_pair), enc_ff_pieces)
    pair_sum = add_short(pair_keep, swap_core(pair_send)).astype(jnp.bfloat16)
    arrived = swap_z(pair_sum, 1)
    own_sum = add_short(own_keep, swap_core(own_send))
    arrived, dec_up, dec_down_t = together(arrived, dec_up, dec_down_t)
    dec_ff = Halved(dec_up, dec_down_t)
    total = (own_sum + arrived.astype(jnp.float32)).astype(jnp.bfloat16)
    total = total.reshape(2, slot_count, model_width)
    total = add_short(pick(total, x, 0), swap_x(pick(total, 1 - x, 0)))
    kept = pick(mid.reshape(2, slot_count, model_width), x, 0)
    encoded = (kept.astype(jnp.float32) + total).astype(jnp.bfloat16)

    encoded, dec_ff.first = together(encoded, dec_ff.first)
    partial_merge = dot_t(encoded, w_merge).astype(jnp.bfloat16)
    partial_merge = partial_merge.reshape(slot_count, 2, half_width)
    merged = add_short(pick(partial_merge, c, 1), swap_core(pick(partial_merge, 1 - c, 1)))
    merged = merged.astype(jnp.bfloat16)
    merged, dec_ff.second = together(merged, dec_ff.second)
    dec_ff.forward()
    merged = add_short(merged, swap_x(merged)).astype(jnp.bfloat16)

    even_share = slot_count // senders
    capacity = even_share + max(even_share // 2, 1)
    padded = -(-capacity // 16) * 16
    one_hot = (dest_dev[:, None] == jnp.arange(senders, dtype=jnp.int32)[None, :]).astype(jnp.int32)
    earlier = jnp.cumsum(one_hot, axis=0) - one_hot
    slot_rank = jnp.sum(earlier * one_hot, axis=1)
    bucket = dest_dev * padded + slot_rank
    chosen = jnp.arange(senders * padded, dtype=jnp.int32)[:, None] == bucket[None, :]
    digits = jnp.stack([slot_valid.astype(jnp.int32), dest_pos // 128, dest_pos % 128], 1)
    digits = jnp.pad(digits, ((0, 0), (0, 125))).astype(jnp.bfloat16)
    outgoing = jnp.dot(
        chosen.astype(jnp.bfloat16),
        jnp.concatenate([merged, digits], axis=1),
        preferred_element_type=jnp.float32,
    ).astype(jnp.bfloat16)
    outgoing, dec_ff.third = together(outgoing, dec_ff.third)
    dec_ff_pieces = dec_ff.pieces()
    incoming = exchange_blocks(outgoing.reshape(8, senders // 8, padded, -1))
    incoming = incoming.reshape(senders * padded, -1)

    seq_len = text_embed.shape[0]
    half_rows = seq_len // 2
    positions = jnp.arange(seq_len, dtype=jnp.int32)
    marks = incoming[:, half_width:].astype(jnp.int32)
    target = jnp.where(marks[:, 0] > 0, marks[:, 1] * 128 + marks[:, 2], -1)
    hits = positions[:, None] == target[None, :]
    placed = jnp.dot(
        hits.astype(jnp.bfloat16), incoming[:, :half_width], preferred_element_type=jnp.float32
    ).astype(jnp.bfloat16)
    text_half = lax.dynamic_slice_in_dim(text_embed, c * half_width, half_width, 1)
    dec_half = jnp.where(jnp.any(hits, axis=1)[:, None], placed, text_half)
    rows = join_core(dec_half, 1)

    causal = (positions[:, None] >= positions[None, :]).astype(jnp.float32)
    keep, send = attention(spots, rows, causal, [w_dec_attn], qkv_width)
    mine = add_short(keep, swap_core(send)).astype(jnp.bfloat16)
    mid, normed = middle(spots, rows, mine, swap_x(mine))
    normed_pair = swap_z(normed, 1)
    own_keep, own_send = feed_forward(spots, normed, swap_core(normed), dec_ff_pieces)
    pair_keep, pair_send = feed_forward(spots, normed_pair, swap_core(normed_pair), dec_ff_pieces)
    pair_sum = add_short(pair_keep, swap_core(pair_send)).astype(jnp.bfloat16)
    arrived = swap_z(pair_sum, 1)
    own_sum = add_short(own_keep, swap_core(own_send))
    total = (own_sum + arrived.astype(jnp.float32)).astype(jnp.bfloat16)
    total = add_short(total, swap_x(total))
    decoded = (mid.astype(jnp.float32) + total).astype(jnp.bfloat16)
    keep_mask = positions < slot_count + text_len[0]
    keep_half = pick(keep_mask.reshape(2, half_rows), c, 0)
    decoded = jnp.where(keep_half[:, None], decoded, jnp.zeros_like(decoded))
    return join_core(decoded, 0)


def solution(mesh):
    return jax.shard_map(
        on_device,
        mesh=mesh,
        in_specs=(
            P("req", None),
            P("req", None),
            P("req", None),
            P("req"),
            P("req"),
            P("req"),
            P("req", "tp"),
            P("req", "tp"),
            P("req", "tp"),
            P("req", "tp"),
            P("req", "tp"),
            P("req", "tp"),
            P("req", "tp"),
            P("req", "tp"),
            P("req", "tp"),
        ),
        out_specs=P("req", None),
        check_vma=False,
    )
```

```python
import jax
import jax.numpy as jnp
from jax import lax
from jax.experimental import pallas as pl
from jax.experimental.pallas import tpu as pltpu
from jax.sharding import PartitionSpec as P

HEAD_DIM = 80
GRID = 16
HALF = GRID // 2
EPS = 1e-06
AXES = ("req", "tp")


def routes(move):
    groups = lax.axis_size("req") // 8
    pairs = []
    for z in range(4):
        for y in range(2):
            for x in range(2):
                for c in range(2):
                    z2, y2, x2, c2 = move(z, y, x, c)
                    for g in range(groups):
                        source = ((z * 2 + y) * groups + g) * 4 + x * 2 + c
                        target = ((z2 * 2 + y2) * groups + g) * 4 + x2 * 2 + c2
                        pairs.append((source, target))
    return pairs


def swap_core(part):
    return lax.ppermute(part, AXES, routes(lambda z, y, x, c: (z, y, x, 1 - c)))


def swap_x(part):
    return lax.ppermute(part, AXES, routes(lambda z, y, x, c: (z, y, 1 - x, c)))


def swap_y(part):
    return lax.ppermute(part, AXES, routes(lambda z, y, x, c: (z, 1 - y, x, c)))


def swap_z(part, k):
    return lax.ppermute(part, AXES, routes(lambda z, y, x, c: (z ^ k, y, x, c)))


def place():
    index = lax.axis_index("req") // (lax.axis_size("req") // 8)
    tensor = lax.axis_index("tp")
    return index // 2, index % 2, tensor // 2, tensor % 2


def own_rows(weight):
    groups = lax.axis_size("req") // 8
    if groups == 1:
        return weight
    members = [[i * groups + g for g in range(groups)] for i in range(8)]
    return lax.all_gather(weight, "req", axis=0, tiled=True, axis_index_groups=members)


def together(*values):
    return lax.optimization_barrier(values)


def halves_by_z(weight):
    z, _, _, _ = place()
    half = weight.shape[1] // 2
    return [
        lax.dynamic_slice_in_dim(weight, ((z % 2) ^ bit) * half, half, 1) for bit in (0, 1)
    ]


class Halved:
    def __init__(self, mine, others, near):
        self.own = mine
        self.first = swap_z(near, 1)
        self.second = swap_z(mine, 2)
        self.third = swap_z(others, 3)
        self.y_own = swap_y(mine)

    def pieces(self):
        column = jnp.concatenate([self.first, self.second, self.third], axis=0)
        column, self.y_own = together(column, self.y_own)
        return [self.own, column, self.y_own, swap_y(column)]


def halved_column(weight):
    groups = lax.axis_size("req") // 8
    half = weight.shape[1] // 2
    members = [
        [(z * 2 + y) * groups + g for z in range(4)] for y in range(2) for g in range(groups)
    ]
    column = lax.all_to_all(
        jnp.stack([weight[:, :half], weight[:, half:]] * 2),
        "req",
        split_axis=0,
        concat_axis=0,
        tiled=True,
        axis_index_groups=members,
    ).reshape(-1, half)
    return [column, swap_y(column)]


def block_places():
    z, y, _, c = place()
    direct = [(z ^ k) * 2 + (y ^ v) for v in range(2) for k in range(4)]
    whole = [(z ^ k) * 2 + (y ^ v) for ks in ((0, 2), (1, 3)) for v in range(2) for k in ks]
    columns = [k * 2 + (y ^ v) for v in range(2) for k in range(4)]
    return jnp.stack(direct + whole + columns + [c]).astype(jnp.int32)


def load_weight(spots, base, pieces, weight, sems):
    height = weight.shape[0] // 8
    copies = []
    for piece in pieces:
        for block in range(piece.shape[0] // height):
            at = len(copies)
            start = pl.multiple_of(spots[base + at] * height, 16)
            copies.append(
                pltpu.make_async_copy(
                    piece.at[pl.ds(block * height, height)],
                    weight.at[pl.ds(start, height)],
                    sems.at[at],
                )
            )
    for copy in copies:
        copy.start()
    return copies


def norm(values_f):
    center = values_f - jnp.mean(values_f, axis=-1, keepdims=True)
    spread = jnp.mean(center * center, axis=-1, keepdims=True)
    return (center * lax.rsqrt(spread + EPS)).astype(jnp.bfloat16)


def dot_t(left, right):
    return lax.dot_general(left, right, (((1,), (1,)), ((), ())), preferred_element_type=jnp.float32)


DIRECT, WHOLE, COLUMNS = 0, 8, 16
VMEM = pl.BlockSpec(memory_space=pltpu.VMEM)
SMEM = pl.BlockSpec(memory_space=pltpu.SMEM)
ANY = pl.BlockSpec(memory_space=pl.ANY)


def local_call(kernel, ins, in_specs, outs, scratch, limit=56):
    return pl.pallas_call(
        kernel,
        in_specs=in_specs,
        out_specs=[VMEM] * len(outs),
        out_shape=[jax.ShapeDtypeStruct(shape, jnp.bfloat16) for shape in outs],
        scratch_shapes=scratch,
        cost_estimate=pl.CostEstimate(flops=0, bytes_accessed=0, transcendentals=0),
        compiler_params=pltpu.CompilerParams(vmem_limit_bytes=limit * 2**20),
    )(*ins)


def attention(spots, base, rows, allowed, pieces, qkv_width):
    length, width = rows.shape
    heads = qkv_width // (3 * HEAD_DIM)
    half = length // 2

    def kernel(spots_ref, rows_ref, allowed_ref, *refs):
        piece_refs = refs[: len(pieces)]
        keep, send, weight, projected, mixed, sems = refs[len(pieces) :]
        copies = load_weight(spots_ref, base, piece_refs, weight, sems)
        normed = norm(rows_ref[...].astype(jnp.float32))
        mixed[...] = jnp.zeros_like(mixed)
        for copy in copies:
            copy.wait()
        projected[...] = (
            jnp.dot(normed, weight[...], preferred_element_type=jnp.float32)
            .astype(jnp.bfloat16)
            .astype(jnp.float32)
        )
        for head in range(heads):
            at = head * 3 * HEAD_DIM
            query = projected[:, at : at + HEAD_DIM].astype(jnp.bfloat16)
            key = projected[:, at + HEAD_DIM : at + 2 * HEAD_DIM].astype(jnp.bfloat16)
            value = projected[:, at + 2 * HEAD_DIM : at + 3 * HEAD_DIM].astype(jnp.bfloat16)
            scores = dot_t(query, key) * HEAD_DIM ** (-0.5)
            scores = jnp.where(allowed_ref[...] > 0, scores, -1e30)
            exponent = jnp.exp(scores - jnp.max(scores, axis=-1, keepdims=True))
            soft = (exponent / jnp.sum(exponent, axis=-1, keepdims=True)).astype(jnp.bfloat16)
            out_at = qkv_width + head * HEAD_DIM
            mixed[:, out_at : out_at + HEAD_DIM] = jnp.dot(
                soft, value, preferred_element_type=jnp.float32
            )
        projected[...] = dot_t(mixed[...].astype(jnp.bfloat16), weight[...])
        core = spots_ref[24]
        keep[...] = projected[pl.ds(pl.multiple_of(core * half, 16), half), :].astype(jnp.bfloat16)
        send[...] = projected[pl.ds(pl.multiple_of((1 - core) * half, 16), half), :].astype(
            jnp.bfloat16
        )

    return local_call(
        kernel,
        [spots, rows, allowed] + pieces,
        [SMEM, VMEM, VMEM] + [ANY] * len(pieces),
        [(half, width)] * 2,
        [
            pltpu.VMEM((width, width), jnp.bfloat16),
            pltpu.VMEM((length, width), jnp.float32),
            pltpu.VMEM((length, width), jnp.float32),
            pltpu.SemaphoreType.DMA((8,)),
        ],
    )


def middle(spots, rows, left, right):
    half, width = left.shape

    def kernel(spots_ref, rows_ref, left_ref, right_ref, mid, normed):
        base = rows_ref[pl.ds(pl.multiple_of(spots_ref[24] * half, 16), half), :]
        total = left_ref[...].astype(jnp.float32) + right_ref[...].astype(jnp.float32)
        value = (base.astype(jnp.float32) + total).astype(jnp.bfloat16)
        mid[...] = value
        normed[...] = norm(value.astype(jnp.float32))

    return local_call(
        kernel, [spots, rows, left, right], [SMEM, VMEM, VMEM, VMEM], [(half, width)] * 2, [], 16
    )


def feed_forward(spots, sources, weights, bases):
    half, width = sources[0].shape
    units = width // 2
    pieces = [piece for weight in weights for piece in weight]
    parts = len(weights)
    rows = len(sources)

    def kernel(spots_ref, *refs):
        source_refs, piece_refs, refs = (
            refs[:rows],
            refs[rows : rows + len(pieces)],
            refs[rows + len(pieces) :],
        )
        targets, scratch = refs[:rows], refs[rows:]
        copies, at = [], 0
        for part in range(parts):
            mine = piece_refs[at : at + len(weights[part])]
            at += len(mine)
            copies += load_weight(spots_ref, bases[part], mine, scratch[part], scratch[parts + part])
        for copy in copies:
            copy.wait()
        if parts == 1:
            up, down = scratch[0][:, :units], scratch[0][:, units:]
        else:
            up, down = scratch[0][...], scratch[1][...]
        for source, target in zip(source_refs, targets):
            hidden = jnp.dot(source[...], up, preferred_element_type=jnp.float32)
            hidden = 0.5 * hidden * (1.0 + lax.erf(hidden * 0.5**0.5))
            target[...] = dot_t(hidden.astype(jnp.bfloat16), down).astype(jnp.bfloat16)

    return local_call(
        kernel,
        [spots] + sources + pieces,
        [SMEM] + [VMEM] * rows + [ANY] * len(pieces),
        [(half, width)] * rows,
        [pltpu.VMEM((width, weight[0].shape[1]), jnp.bfloat16) for weight in weights]
        + [pltpu.SemaphoreType.DMA((8,))] * parts,
    )


def merge(spots, base, blocks, pieces):
    count, width = blocks.shape
    half = width // 2

    def kernel(spots_ref, blocks_ref, *refs):
        piece_refs = refs[: len(pieces)]
        keep, send, weight, sems = refs[len(pieces) :]
        for copy in load_weight(spots_ref, base, piece_refs, weight, sems):
            copy.wait()
        core = spots_ref[24]
        source = blocks_ref[...]
        for side, target in ((core, keep), (1 - core, send)):
            rows = weight[pl.ds(pl.multiple_of(side * half, 16), half), :]
            target[...] = dot_t(source, rows).astype(jnp.bfloat16)

    return local_call(
        kernel,
        [spots, blocks] + pieces,
        [SMEM, VMEM] + [ANY] * len(pieces),
        [(count, half)] * 2,
        [pltpu.VMEM((width, width), jnp.bfloat16), pltpu.SemaphoreType.DMA((8,))],
    )


def pick(rows, which, axis):
    return lax.dynamic_index_in_dim(rows, which, axis, keepdims=False)


def add_short(left, right):
    return left.astype(jnp.float32) + right.astype(jnp.float32)


def join_core(half, axis):
    _, _, _, c = place()
    other = swap_core(half)
    first = jnp.where(c == 0, half, other)
    second = jnp.where(c == 0, other, half)
    return jnp.concatenate([first, second], axis=axis)


def exchange_y(blocks):
    _, y, _, _ = place()
    groups = blocks.shape[1]
    if groups > 1:
        members = [[i * groups + g for g in range(groups)] for i in range(8)]
        blocks = lax.all_to_all(
            blocks, "req", split_axis=1, concat_axis=1, tiled=True, axis_index_groups=members
        )
    blocks = blocks.reshape((4, 2) + blocks.shape[1:])
    return jnp.stack([pick(blocks, y, 1), swap_y(pick(blocks, 1 - y, 1))], axis=1)


def exchange_z(both):
    z, _, _, _ = place()
    mixed = [pick(both, z, 0)] + [swap_z(pick(both, z ^ k, 0), k) for k in (1, 2, 3)]
    return jnp.concatenate(mixed, axis=0)


def on_device(
    patches,
    half_grid,
    text_embed,
    dest_dev,
    dest_pos,
    text_len,
    enc_qkv,
    enc_out_t,
    enc_up,
    enc_down_t,
    merge_t,
    dec_qkv,
    dec_out_t,
    dec_up,
    dec_down_t,
):
    _, _, x, c = place()
    senders = lax.axis_size("req")
    image_count = half_grid.shape[0]
    model_width = patches.shape[1]
    cells = HALF * HALF
    slot_count = image_count * cells
    qkv_width = enc_qkv.shape[1]
    half_width = model_width // 2
    spots = block_places()

    enc_attn = own_rows(jnp.concatenate([enc_qkv, enc_out_t], axis=1))
    enc_up, enc_down_t = own_rows(enc_up), own_rows(enc_down_t)
    merge_t = own_rows(merge_t)
    dec_attn = own_rows(jnp.concatenate([dec_qkv, dec_out_t], axis=1))
    dec_up, dec_down_t = own_rows(dec_up), own_rows(dec_down_t)

    first, second, y_own = swap_z(enc_attn, 1), swap_z(enc_attn, 2), swap_y(enc_attn)
    first, second, y_own, enc_up, enc_down_t = together(first, second, y_own, enc_up, enc_down_t)
    third = swap_z(second, 1)
    y_early = swap_y(jnp.concatenate([first, second], axis=0))

    up, down = halves_by_z(enc_up), halves_by_z(enc_down_t)
    mine, others = [jnp.concatenate(pair, axis=1) for pair in zip(up, down)]
    third, near = together(third, others)
    enc_ff = Halved(mine, others, near)
    enc_attn = [enc_attn, first, second, third, y_own, y_early, swap_y(third)]
    enc_ff.third, merge_t = together(enc_ff.third, merge_t)
    enc_ff = enc_ff.pieces()

    merge_second = swap_z(merge_t, 2)

    cell_index = jnp.arange(cells, dtype=jnp.int32)
    slot_valid = ((cell_index // HALF)[None, :] < half_grid[:, 0:1]) & (
        (cell_index % HALF)[None, :] < half_grid[:, 1:2]
    )
    slot_valid = slot_valid.reshape(-1)

    rows = patches.reshape(image_count, HALF, 2, HALF, 2, model_width)
    rows = rows.transpose(4, 2, 0, 1, 3, 5).reshape(4 * slot_count, model_width)
    image_of = jnp.tile(jnp.arange(slot_count, dtype=jnp.int32) // cells, 4)
    allowed = (image_of[:, None] == image_of[None, :]) & jnp.tile(slot_valid, 4)[None, :]
    allowed = allowed.astype(jnp.float32)

    keep, send = attention(spots, DIRECT, rows, allowed, enc_attn, qkv_width)
    mine = add_short(keep, swap_core(send)).astype(jnp.bfloat16)
    mid, normed = middle(spots, rows, mine, swap_x(mine))
    normed, merge_second = together(normed, merge_second)
    normed_pair = swap_z(normed, 1)
    sources = [normed, swap_core(normed), normed_pair, swap_core(normed_pair)]
    merge_two = jnp.concatenate([merge_t, merge_second], axis=0)
    merge_pair = swap_z(merge_two, 1)
    merge_two_y = swap_y(merge_two)
    own_keep, own_send, pair_keep, pair_send = feed_forward(spots, sources, [enc_ff], [DIRECT])
    pair_sum = add_short(pair_keep, swap_core(pair_send)).astype(jnp.bfloat16)
    pair_sum, merge_pair, merge_two_y, dec_attn = together(
        pair_sum, merge_pair, merge_two_y, dec_attn
    )
    arrived = swap_z(pair_sum, 1)
    attn_second = swap_z(dec_attn, 2)
    merge_all = [merge_two, merge_two_y, merge_pair, swap_y(merge_pair)]
    own_sum = add_short(own_keep, swap_core(own_send))
    total = (own_sum + arrived.astype(jnp.float32)).astype(jnp.bfloat16)
    total = total.reshape(2, slot_count, model_width)
    total = add_short(pick(total, x, 0), swap_x(pick(total, 1 - x, 0)))
    kept = pick(mid.reshape(2, slot_count, model_width), x, 0)
    encoded = (kept.astype(jnp.float32) + total).astype(jnp.bfloat16)

    encoded, attn_second = together(encoded, attn_second)
    attn_two = jnp.concatenate([dec_attn, attn_second], axis=0)
    attn_pair = swap_z(attn_two, 1)
    attn_two_y = swap_y(attn_two)
    keep, send = merge(spots, WHOLE, encoded, merge_all)
    merged = add_short(keep, swap_core(send))
    merged = merged.astype(jnp.bfloat16)
    merged = add_short(merged, swap_x(merged)).astype(jnp.bfloat16)

    even_share = slot_count // senders
    capacity = even_share + max(even_share // 2, 1)
    padded = -(-capacity // 16) * 16
    one_hot = (dest_dev[:, None] == jnp.arange(senders, dtype=jnp.int32)[None, :]).astype(jnp.int32)
    earlier = jnp.cumsum(one_hot, axis=0) - one_hot
    slot_rank = jnp.sum(earlier * one_hot, axis=1)
    bucket = dest_dev * padded + slot_rank
    chosen = jnp.arange(senders * padded, dtype=jnp.int32)[:, None] == bucket[None, :]
    digits = jnp.stack([slot_valid.astype(jnp.int32), dest_pos // 128, dest_pos % 128], 1)
    digits = jnp.pad(digits, ((0, 0), (0, 125))).astype(jnp.bfloat16)
    outgoing = jnp.dot(
        chosen.astype(jnp.bfloat16),
        jnp.concatenate([merged, digits], axis=1),
        preferred_element_type=jnp.float32,
    ).astype(jnp.bfloat16)
    outgoing, attn_pair, attn_two_y, dec_up = together(outgoing, attn_pair, attn_two_y, dec_up)
    mine, others = halves_by_z(dec_up)
    dec_up = Halved(mine, others, others)
    both = exchange_y(outgoing.reshape(8, senders // 8, padded, -1))
    both, attn_pair = together(both, attn_pair)
    both, dec_up.first, dec_up.second, dec_up.third = together(
        both, dec_up.first, dec_up.second, dec_up.third
    )
    dec_up = dec_up.pieces()
    dec_attn = [attn_two, attn_two_y, attn_pair, swap_y(attn_pair)]
    incoming = exchange_z(both)
    incoming, dec_down_t = together(incoming, dec_down_t)
    dec_down = halved_column(dec_down_t)
    incoming = incoming.reshape(senders * padded, -1)

    seq_len = text_embed.shape[0]
    half_rows = seq_len // 2
    positions = jnp.arange(seq_len, dtype=jnp.int32)
    marks = incoming[:, half_width:].astype(jnp.int32)
    target = jnp.where(marks[:, 0] > 0, marks[:, 1] * 128 + marks[:, 2], -1)
    hits = positions[:, None] == target[None, :]
    placed = jnp.dot(
        hits.astype(jnp.bfloat16), incoming[:, :half_width], preferred_element_type=jnp.float32
    ).astype(jnp.bfloat16)
    text_half = lax.dynamic_slice_in_dim(text_embed, c * half_width, half_width, 1)
    dec_half = jnp.where(jnp.any(hits, axis=1)[:, None], placed, text_half)
    rows = join_core(dec_half, 1)
    causal = (positions[:, None] >= positions[None, :]).astype(jnp.float32)
    keep, send = attention(spots, WHOLE, rows, causal, dec_attn, qkv_width)
    mine = add_short(keep, swap_core(send)).astype(jnp.bfloat16)
    mine, *dec_up = together(mine, *dec_up)
    mid, normed = middle(spots, rows, mine, swap_x(mine))
    normed_pair = swap_z(normed, 1)
    sources = [normed, swap_core(normed), normed_pair, swap_core(normed_pair)]
    own_keep, own_send, pair_keep, pair_send = feed_forward(spots, sources, [dec_up, dec_down], [DIRECT, COLUMNS])
    pair_sum = add_short(pair_keep, swap_core(pair_send)).astype(jnp.bfloat16)
    arrived = swap_z(pair_sum, 1)
    own_sum = add_short(own_keep, swap_core(own_send))
    total = (own_sum + arrived.astype(jnp.float32)).astype(jnp.bfloat16)
    total = add_short(total, swap_x(total))
    decoded = (mid.astype(jnp.float32) + total).astype(jnp.bfloat16)
    keep_mask = positions < slot_count + text_len[0]
    keep_half = pick(keep_mask.reshape(2, half_rows), c, 0)
    decoded = jnp.where(keep_half[:, None], decoded, jnp.zeros_like(decoded))
    return join_core(decoded, 0)


def solution(mesh):
    return jax.shard_map(
        on_device,
        mesh=mesh,
        in_specs=(
            P("req", None),
            P("req", None),
            P("req", None),
            P("req"),
            P("req"),
            P("req"),
            P("req", "tp"),
            P("req", "tp"),
            P("req", "tp"),
            P("req", "tp"),
            P("req", "tp"),
            P("req", "tp"),
            P("req", "tp"),
            P("req", "tp"),
            P("req", "tp"),
        ),
        out_specs=P("req", None),
        check_vma=False,
    )
```

```python
import jax
import jax.numpy as jnp
from jax import lax
from jax.experimental import pallas as pl
from jax.experimental.pallas import tpu as pltpu
from jax.sharding import PartitionSpec as P

HEAD_DIM = 80
GRID = 16
HALF = GRID // 2
EPS = 1e-06
AXES = ("req", "tp")


def routes(move):
    groups = lax.axis_size("req") // 8
    pairs = []
    for z in range(4):
        for y in range(2):
            for x in range(2):
                for c in range(2):
                    z2, y2, x2, c2 = move(z, y, x, c)
                    for g in range(groups):
                        source = ((z * 2 + y) * groups + g) * 4 + x * 2 + c
                        target = ((z2 * 2 + y2) * groups + g) * 4 + x2 * 2 + c2
                        pairs.append((source, target))
    return pairs


def swap_core(part):
    return lax.ppermute(part, AXES, routes(lambda z, y, x, c: (z, y, x, 1 - c)))


def swap_x(part):
    return lax.ppermute(part, AXES, routes(lambda z, y, x, c: (z, y, 1 - x, c)))


def swap_y(part):
    return lax.ppermute(part, AXES, routes(lambda z, y, x, c: (z, 1 - y, x, c)))


def swap_z(part, k):
    return lax.ppermute(part, AXES, routes(lambda z, y, x, c: (z ^ k, y, x, c)))


def place():
    index = lax.axis_index("req") // (lax.axis_size("req") // 8)
    tensor = lax.axis_index("tp")
    return index // 2, index % 2, tensor // 2, tensor % 2


def own_rows(weight):
    groups = lax.axis_size("req") // 8
    if groups == 1:
        return weight
    members = [[i * groups + g for g in range(groups)] for i in range(8)]
    return lax.all_gather(weight, "req", axis=0, tiled=True, axis_index_groups=members)


def together(*values):
    return lax.optimization_barrier(values)


def halves_by_z(weight):
    z, _, _, _ = place()
    half = weight.shape[1] // 2
    return [
        lax.dynamic_slice_in_dim(weight, ((z % 2) ^ bit) * half, half, 1) for bit in (0, 1)
    ]


class Halved:
    def __init__(self, mine, others, near):
        self.own = mine
        self.first = swap_z(near, 1)
        self.second = swap_z(mine, 2)
        self.third = swap_z(others, 3)
        self.y_own = swap_y(mine)

    def pieces(self):
        column = jnp.concatenate([self.first, self.second, self.third], axis=0)
        column, self.y_own = together(column, self.y_own)
        return [self.own, column, self.y_own, swap_y(column)]


def halved_column(weight):
    groups = lax.axis_size("req") // 8
    half = weight.shape[1] // 2
    members = [
        [(z * 2 + y) * groups + g for z in range(4)] for y in range(2) for g in range(groups)
    ]
    column = lax.all_to_all(
        jnp.stack([weight[:, :half], weight[:, half:]] * 2),
        "req",
        split_axis=0,
        concat_axis=0,
        tiled=True,
        axis_index_groups=members,
    ).reshape(-1, half)
    return [column, swap_y(column)]


def block_places():
    z, y, _, c = place()
    direct = [(z ^ k) * 2 + (y ^ v) for v in range(2) for k in range(4)]
    whole = [(z ^ k) * 2 + (y ^ v) for ks in ((0, 2), (1, 3)) for v in range(2) for k in ks]
    columns = [k * 2 + (y ^ v) for v in range(2) for k in range(4)]
    return jnp.stack(direct + whole + columns + [c]).astype(jnp.int32)


def load_weight(spots, base, pieces, weight, sems):
    height = weight.shape[0] // 8
    copies = []
    for piece in pieces:
        for block in range(piece.shape[0] // height):
            at = len(copies)
            start = pl.multiple_of(spots[base + at] * height, 16)
            copies.append(
                pltpu.make_async_copy(
                    piece.at[pl.ds(block * height, height)],
                    weight.at[pl.ds(start, height)],
                    sems.at[at],
                )
            )
    for copy in copies:
        copy.start()
    return copies


def norm(values_f):
    center = values_f - jnp.mean(values_f, axis=-1, keepdims=True)
    spread = jnp.mean(center * center, axis=-1, keepdims=True)
    return (center * lax.rsqrt(spread + EPS)).astype(jnp.bfloat16)


def dot_t(left, right):
    return lax.dot_general(left, right, (((1,), (1,)), ((), ())), preferred_element_type=jnp.float32)


DIRECT, WHOLE, COLUMNS = 0, 8, 16
VMEM = pl.BlockSpec(memory_space=pltpu.VMEM)
SMEM = pl.BlockSpec(memory_space=pltpu.SMEM)
ANY = pl.BlockSpec(memory_space=pl.ANY)


def local_call(kernel, ins, in_specs, outs, scratch, limit=56):
    return pl.pallas_call(
        kernel,
        in_specs=in_specs,
        out_specs=[VMEM] * len(outs),
        out_shape=[jax.ShapeDtypeStruct(shape, jnp.bfloat16) for shape in outs],
        scratch_shapes=scratch,
        cost_estimate=pl.CostEstimate(flops=0, bytes_accessed=0, transcendentals=0),
        compiler_params=pltpu.CompilerParams(vmem_limit_bytes=limit * 2**20),
    )(*ins)


def attention(spots, base, rows, allowed, pieces, qkv_width):
    length, width = rows.shape
    heads = qkv_width // (3 * HEAD_DIM)
    half = length // 2

    def kernel(spots_ref, rows_ref, allowed_ref, *refs):
        piece_refs = refs[: len(pieces)]
        keep, send, weight, projected, mixed, sems = refs[len(pieces) :]
        copies = load_weight(spots_ref, base, piece_refs, weight, sems)
        normed = norm(rows_ref[...].astype(jnp.float32))
        mixed[...] = jnp.zeros_like(mixed)
        for copy in copies:
            copy.wait()
        projected[...] = (
            jnp.dot(normed, weight[...], preferred_element_type=jnp.float32)
            .astype(jnp.bfloat16)
            .astype(jnp.float32)
        )
        for head in range(heads):
            at = head * 3 * HEAD_DIM
            query = projected[:, at : at + HEAD_DIM].astype(jnp.bfloat16)
            key = projected[:, at + HEAD_DIM : at + 2 * HEAD_DIM].astype(jnp.bfloat16)
            value = projected[:, at + 2 * HEAD_DIM : at + 3 * HEAD_DIM].astype(jnp.bfloat16)
            scores = dot_t(query, key) * HEAD_DIM ** (-0.5)
            scores = jnp.where(allowed_ref[...] > 0, scores, -1e30)
            exponent = jnp.exp(scores - jnp.max(scores, axis=-1, keepdims=True))
            soft = (exponent / jnp.sum(exponent, axis=-1, keepdims=True)).astype(jnp.bfloat16)
            out_at = qkv_width + head * HEAD_DIM
            mixed[:, out_at : out_at + HEAD_DIM] = jnp.dot(
                soft, value, preferred_element_type=jnp.float32
            )
        projected[...] = dot_t(mixed[...].astype(jnp.bfloat16), weight[...])
        core = spots_ref[24]
        keep[...] = projected[pl.ds(pl.multiple_of(core * half, 16), half), :].astype(jnp.bfloat16)
        send[...] = projected[pl.ds(pl.multiple_of((1 - core) * half, 16), half), :].astype(
            jnp.bfloat16
        )

    return local_call(
        kernel,
        [spots, rows, allowed] + pieces,
        [SMEM, VMEM, VMEM] + [ANY] * len(pieces),
        [(half, width)] * 2,
        [
            pltpu.VMEM((width, width), jnp.bfloat16),
            pltpu.VMEM((length, width), jnp.float32),
            pltpu.VMEM((length, width), jnp.float32),
            pltpu.SemaphoreType.DMA((8,)),
        ],
    )


def middle(spots, rows, left, right):
    half, width = left.shape

    def kernel(spots_ref, rows_ref, left_ref, right_ref, mid, normed):
        base = rows_ref[pl.ds(pl.multiple_of(spots_ref[24] * half, 16), half), :]
        total = left_ref[...].astype(jnp.float32) + right_ref[...].astype(jnp.float32)
        value = (base.astype(jnp.float32) + total).astype(jnp.bfloat16)
        mid[...] = value
        normed[...] = norm(value.astype(jnp.float32))

    return local_call(
        kernel, [spots, rows, left, right], [SMEM, VMEM, VMEM, VMEM], [(half, width)] * 2, [], 16
    )


def feed_forward(spots, sources, weights, bases):
    half, width = sources[0].shape
    units = width // 2
    pieces = [piece for weight in weights for piece in weight]
    parts = len(weights)
    rows = len(sources)

    def kernel(spots_ref, *refs):
        source_refs, piece_refs, refs = (
            refs[:rows],
            refs[rows : rows + len(pieces)],
            refs[rows + len(pieces) :],
        )
        targets, scratch = refs[:rows], refs[rows:]
        copies, at = [], 0
        for part in range(parts):
            mine = piece_refs[at : at + len(weights[part])]
            at += len(mine)
            copies += load_weight(spots_ref, bases[part], mine, scratch[part], scratch[parts + part])
        for copy in copies:
            copy.wait()
        if parts == 1:
            up, down = scratch[0][:, :units], scratch[0][:, units:]
        else:
            up, down = scratch[0][...], scratch[1][...]
        for source, target in zip(source_refs, targets):
            hidden = jnp.dot(source[...], up, preferred_element_type=jnp.float32)
            hidden = 0.5 * hidden * (1.0 + lax.erf(hidden * 0.5**0.5))
            target[...] = dot_t(hidden.astype(jnp.bfloat16), down).astype(jnp.bfloat16)

    return local_call(
        kernel,
        [spots] + sources + pieces,
        [SMEM] + [VMEM] * rows + [ANY] * len(pieces),
        [(half, width)] * rows,
        [pltpu.VMEM((width, weight[0].shape[1]), jnp.bfloat16) for weight in weights]
        + [pltpu.SemaphoreType.DMA((8,))] * parts,
    )


def merge(spots, base, blocks, pieces):
    count, width = blocks.shape
    half = width // 2

    def kernel(spots_ref, blocks_ref, *refs):
        piece_refs = refs[: len(pieces)]
        keep, send, weight, sems = refs[len(pieces) :]
        for copy in load_weight(spots_ref, base, piece_refs, weight, sems):
            copy.wait()
        core = spots_ref[24]
        source = blocks_ref[...]
        for side, target in ((core, keep), (1 - core, send)):
            rows = weight[pl.ds(pl.multiple_of(side * half, 16), half), :]
            target[...] = dot_t(source, rows).astype(jnp.bfloat16)

    return local_call(
        kernel,
        [spots, blocks] + pieces,
        [SMEM, VMEM] + [ANY] * len(pieces),
        [(count, half)] * 2,
        [pltpu.VMEM((width, width), jnp.bfloat16), pltpu.SemaphoreType.DMA((8,))],
    )


def pick(rows, which, axis):
    return lax.dynamic_index_in_dim(rows, which, axis, keepdims=False)


def add_short(left, right):
    return left.astype(jnp.float32) + right.astype(jnp.float32)


def join_core(half, axis):
    _, _, _, c = place()
    other = swap_core(half)
    first = jnp.where(c == 0, half, other)
    second = jnp.where(c == 0, other, half)
    return jnp.concatenate([first, second], axis=axis)


def exchange_y(blocks):
    _, y, _, _ = place()
    groups = blocks.shape[1]
    if groups > 1:
        members = [[i * groups + g for g in range(groups)] for i in range(8)]
        blocks = lax.all_to_all(
            blocks, "req", split_axis=1, concat_axis=1, tiled=True, axis_index_groups=members
        )
    blocks = blocks.reshape((4, 2) + blocks.shape[1:])
    return jnp.stack([pick(blocks, y, 1), swap_y(pick(blocks, 1 - y, 1))], axis=1)


def exchange_z(both):
    z, _, _, _ = place()
    mixed = [pick(both, z, 0)] + [swap_z(pick(both, z ^ k, 0), k) for k in (1, 2, 3)]
    return jnp.concatenate(mixed, axis=0)


def on_device(
    patches,
    half_grid,
    text_embed,
    dest_dev,
    dest_pos,
    text_len,
    enc_qkv,
    enc_out_t,
    enc_up,
    enc_down_t,
    merge_t,
    dec_qkv,
    dec_out_t,
    dec_up,
    dec_down_t,
):
    _, _, x, c = place()
    senders = lax.axis_size("req")
    image_count = half_grid.shape[0]
    model_width = patches.shape[1]
    cells = HALF * HALF
    slot_count = image_count * cells
    qkv_width = enc_qkv.shape[1]
    half_width = model_width // 2
    spots = block_places()

    enc_attn = own_rows(jnp.concatenate([enc_qkv, enc_out_t], axis=1))
    enc_up, enc_down_t = own_rows(enc_up), own_rows(enc_down_t)
    merge_t = own_rows(merge_t)
    dec_attn = own_rows(jnp.concatenate([dec_qkv, dec_out_t], axis=1))
    dec_up, dec_down_t = own_rows(dec_up), own_rows(dec_down_t)

    first, second, y_own = swap_z(enc_attn, 1), swap_z(enc_attn, 2), swap_y(enc_attn)
    first, second, y_own, enc_up, enc_down_t = together(first, second, y_own, enc_up, enc_down_t)
    third = swap_z(second, 1)
    y_early = swap_y(jnp.concatenate([first, second], axis=0))

    up, down = halves_by_z(enc_up), halves_by_z(enc_down_t)
    mine, others = [jnp.concatenate(pair, axis=1) for pair in zip(up, down)]
    third, near = together(third, others)
    enc_ff = Halved(mine, others, near)
    enc_attn = [enc_attn, first, second, third, y_own, y_early, swap_y(third)]
    enc_ff.third, merge_t = together(enc_ff.third, merge_t)
    enc_ff = enc_ff.pieces()

    merge_second = swap_z(merge_t, 2)

    cell_index = jnp.arange(cells, dtype=jnp.int32)
    slot_valid = ((cell_index // HALF)[None, :] < half_grid[:, 0:1]) & (
        (cell_index % HALF)[None, :] < half_grid[:, 1:2]
    )
    slot_valid = slot_valid.reshape(-1)

    rows = patches.reshape(image_count, HALF, 2, HALF, 2, model_width)
    rows = rows.transpose(4, 2, 0, 1, 3, 5).reshape(4 * slot_count, model_width)
    image_of = jnp.tile(jnp.arange(slot_count, dtype=jnp.int32) // cells, 4)
    allowed = (image_of[:, None] == image_of[None, :]) & jnp.tile(slot_valid, 4)[None, :]
    allowed = allowed.astype(jnp.float32)

    keep, send = attention(spots, DIRECT, rows, allowed, enc_attn, qkv_width)
    mine = add_short(keep, swap_core(send)).astype(jnp.bfloat16)
    mid, normed = middle(spots, rows, mine, swap_x(mine))
    normed, merge_second = together(normed, merge_second)
    normed_pair = swap_z(normed, 1)
    sources = [normed, swap_core(normed), normed_pair, swap_core(normed_pair)]
    merge_two = jnp.concatenate([merge_t, merge_second], axis=0)
    merge_pair = swap_z(merge_two, 1)
    merge_two_y = swap_y(merge_two)
    own_keep, own_send, pair_keep, pair_send = feed_forward(spots, sources, [enc_ff], [DIRECT])
    pair_sum = add_short(pair_keep, swap_core(pair_send)).astype(jnp.bfloat16)
    pair_sum, merge_pair, merge_two_y, dec_attn = together(
        pair_sum, merge_pair, merge_two_y, dec_attn
    )
    arrived = swap_z(pair_sum, 1)
    attn_second = swap_z(dec_attn, 2)
    merge_all = [merge_two, merge_two_y, merge_pair, swap_y(merge_pair)]
    own_sum = add_short(own_keep, swap_core(own_send))
    total = (own_sum + arrived.astype(jnp.float32)).astype(jnp.bfloat16)
    total = total.reshape(2, slot_count, model_width)
    total = add_short(pick(total, x, 0), swap_x(pick(total, 1 - x, 0)))
    kept = pick(mid.reshape(2, slot_count, model_width), x, 0)
    encoded = (kept.astype(jnp.float32) + total).astype(jnp.bfloat16)

    encoded, attn_second = together(encoded, attn_second)
    attn_two = jnp.concatenate([dec_attn, attn_second], axis=0)
    attn_pair = swap_z(attn_two, 1)
    attn_two_y = swap_y(attn_two)
    keep, send = merge(spots, WHOLE, encoded, merge_all)
    merged = add_short(keep, swap_core(send))
    merged = merged.astype(jnp.bfloat16)
    merged = add_short(merged, swap_x(merged)).astype(jnp.bfloat16)

    even_share = slot_count // senders
    capacity = even_share + max(even_share // 2, 1)
    padded = -(-capacity // 16) * 16
    one_hot = (dest_dev[:, None] == jnp.arange(senders, dtype=jnp.int32)[None, :]).astype(jnp.int32)
    earlier = jnp.cumsum(one_hot, axis=0) - one_hot
    slot_rank = jnp.sum(earlier * one_hot, axis=1)
    bucket = dest_dev * padded + slot_rank
    chosen = jnp.arange(senders * padded, dtype=jnp.int32)[:, None] == bucket[None, :]
    digits = jnp.stack([slot_valid.astype(jnp.int32), dest_pos // 128, dest_pos % 128], 1)
    digits = jnp.pad(digits, ((0, 0), (0, 125))).astype(jnp.bfloat16)
    outgoing = jnp.dot(
        chosen.astype(jnp.bfloat16),
        jnp.concatenate([merged, digits], axis=1),
        preferred_element_type=jnp.float32,
    ).astype(jnp.bfloat16)
    outgoing, attn_pair, attn_two_y, dec_up = together(outgoing, attn_pair, attn_two_y, dec_up)
    mine, others = halves_by_z(dec_up)
    dec_up = Halved(mine, others, others)
    both = exchange_y(outgoing.reshape(8, senders // 8, padded, -1))
    both, attn_pair = together(both, attn_pair)
    both, dec_up.first, dec_up.second, dec_up.third = together(
        both, dec_up.first, dec_up.second, dec_up.third
    )
    dec_up = dec_up.pieces()
    attn_pair_y = swap_y(attn_pair)
    incoming = exchange_z(both)
    incoming, attn_pair_y, dec_down_t = together(incoming, attn_pair_y, dec_down_t)
    dec_attn = [attn_two, attn_two_y, attn_pair, attn_pair_y]
    dec_down = halved_column(dec_down_t)
    incoming = incoming.reshape(senders * padded, -1)

    seq_len = text_embed.shape[0]
    half_rows = seq_len // 2
    positions = jnp.arange(seq_len, dtype=jnp.int32)
    marks = incoming[:, half_width:].astype(jnp.int32)
    target = jnp.where(marks[:, 0] > 0, marks[:, 1] * 128 + marks[:, 2], -1)
    hits = positions[:, None] == target[None, :]
    placed = jnp.dot(
        hits.astype(jnp.bfloat16), incoming[:, :half_width], preferred_element_type=jnp.float32
    ).astype(jnp.bfloat16)
    text_half = lax.dynamic_slice_in_dim(text_embed, c * half_width, half_width, 1)
    dec_half = jnp.where(jnp.any(hits, axis=1)[:, None], placed, text_half)
    dec_half, *dec_up = together(dec_half, *dec_up)
    rows = join_core(dec_half, 1)
    causal = (positions[:, None] >= positions[None, :]).astype(jnp.float32)
    keep, send = attention(spots, WHOLE, rows, causal, dec_attn, qkv_width)
    mine = add_short(keep, swap_core(send)).astype(jnp.bfloat16)
    mid, normed = middle(spots, rows, mine, swap_x(mine))
    normed_pair = swap_z(normed, 1)
    sources = [normed, swap_core(normed), normed_pair, swap_core(normed_pair)]
    own_keep, own_send, pair_keep, pair_send = feed_forward(spots, sources, [dec_up, dec_down], [DIRECT, COLUMNS])
    pair_sum = add_short(pair_keep, swap_core(pair_send)).astype(jnp.bfloat16)
    arrived = swap_z(pair_sum, 1)
    own_sum = add_short(own_keep, swap_core(own_send))
    total = (own_sum + arrived.astype(jnp.float32)).astype(jnp.bfloat16)
    total = add_short(total, swap_x(total))
    decoded = (mid.astype(jnp.float32) + total).astype(jnp.bfloat16)
    keep_mask = positions < slot_count + text_len[0]
    keep_half = pick(keep_mask.reshape(2, half_rows), c, 0)
    decoded = jnp.where(keep_half[:, None], decoded, jnp.zeros_like(decoded))
    return join_core(decoded, 0)


def solution(mesh):
    return jax.shard_map(
        on_device,
        mesh=mesh,
        in_specs=(
            P("req", None),
            P("req", None),
            P("req", None),
            P("req"),
            P("req"),
            P("req"),
            P("req", "tp"),
            P("req", "tp"),
            P("req", "tp"),
            P("req", "tp"),
            P("req", "tp"),
            P("req", "tp"),
            P("req", "tp"),
            P("req", "tp"),
            P("req", "tp"),
        ),
        out_specs=P("req", None),
        check_vma=False,
    )
```

```python
import jax
import jax.numpy as jnp
from jax import lax
from jax.experimental import pallas as pl
from jax.experimental.pallas import tpu as pltpu
from jax.sharding import PartitionSpec as P

HEAD_DIM = 80
GRID = 16
HALF = GRID // 2
EPS = 1e-06
AXES = ("req", "tp")


def routes(move):
    groups = lax.axis_size("req") // 8
    pairs = []
    for z in range(4):
        for y in range(2):
            for x in range(2):
                for c in range(2):
                    z2, y2, x2, c2 = move(z, y, x, c)
                    for g in range(groups):
                        source = ((z * 2 + y) * groups + g) * 4 + x * 2 + c
                        target = ((z2 * 2 + y2) * groups + g) * 4 + x2 * 2 + c2
                        pairs.append((source, target))
    return pairs


def swap_core(part):
    return lax.ppermute(part, AXES, routes(lambda z, y, x, c: (z, y, x, 1 - c)))


def swap_x(part):
    return lax.ppermute(part, AXES, routes(lambda z, y, x, c: (z, y, 1 - x, c)))


def swap_y(part):
    return lax.ppermute(part, AXES, routes(lambda z, y, x, c: (z, 1 - y, x, c)))


def swap_z(part, k):
    return lax.ppermute(part, AXES, routes(lambda z, y, x, c: (z ^ k, y, x, c)))


def place():
    index = lax.axis_index("req") // (lax.axis_size("req") // 8)
    tensor = lax.axis_index("tp")
    return index // 2, index % 2, tensor // 2, tensor % 2


def own_rows(weight):
    groups = lax.axis_size("req") // 8
    if groups == 1:
        return weight
    members = [[i * groups + g for g in range(groups)] for i in range(8)]
    return lax.all_gather(weight, "req", axis=0, tiled=True, axis_index_groups=members)


def together(*values):
    return lax.optimization_barrier(values)


def halves_by_z(weight):
    z, _, _, _ = place()
    half = weight.shape[1] // 2
    return [
        lax.dynamic_slice_in_dim(weight, ((z % 2) ^ bit) * half, half, 1) for bit in (0, 1)
    ]


class Halved:
    def __init__(self, mine, others, near):
        self.own = mine
        self.first = swap_z(near, 1)
        self.second = swap_z(mine, 2)
        self.third = swap_z(others, 3)
        self.y_own = swap_y(mine)

    def pieces(self):
        column = jnp.concatenate([self.first, self.second, self.third], axis=0)
        column, self.y_own = together(column, self.y_own)
        return [self.own, column, self.y_own, swap_y(column)]


def halved_column(weight):
    groups = lax.axis_size("req") // 8
    half = weight.shape[1] // 2
    members = [
        [(z * 2 + y) * groups + g for z in range(4)] for y in range(2) for g in range(groups)
    ]
    column = lax.all_to_all(
        jnp.stack([weight[:, :half], weight[:, half:]] * 2),
        "req",
        split_axis=0,
        concat_axis=0,
        tiled=True,
        axis_index_groups=members,
    ).reshape(-1, half)
    return [column, swap_y(column)]


def block_places():
    z, y, _, c = place()
    direct = [(z ^ k) * 2 + (y ^ v) for v in range(2) for k in range(4)]
    whole = [(z ^ k) * 2 + (y ^ v) for ks in ((0, 2), (1, 3)) for v in range(2) for k in ks]
    columns = [k * 2 + (y ^ v) for v in range(2) for k in range(4)]
    return jnp.stack(direct + whole + columns + [c]).astype(jnp.int32)


def load_weight(spots, base, pieces, weight, sems):
    height = weight.shape[0] // 8
    copies = []
    for piece in pieces:
        for block in range(piece.shape[0] // height):
            at = len(copies)
            start = pl.multiple_of(spots[base + at] * height, 16)
            copies.append(
                pltpu.make_async_copy(
                    piece.at[pl.ds(block * height, height)],
                    weight.at[pl.ds(start, height)],
                    sems.at[at],
                )
            )
    for copy in copies:
        copy.start()
    return copies


def norm(values_f):
    center = values_f - jnp.mean(values_f, axis=-1, keepdims=True)
    spread = jnp.mean(center * center, axis=-1, keepdims=True)
    return (center * lax.rsqrt(spread + EPS)).astype(jnp.bfloat16)


def dot_t(left, right):
    return lax.dot_general(left, right, (((1,), (1,)), ((), ())), preferred_element_type=jnp.float32)


DIRECT, WHOLE, COLUMNS = 0, 8, 16
VMEM = pl.BlockSpec(memory_space=pltpu.VMEM)
SMEM = pl.BlockSpec(memory_space=pltpu.SMEM)
ANY = pl.BlockSpec(memory_space=pl.ANY)


def local_call(kernel, ins, in_specs, outs, scratch, limit=28):
    return pl.pallas_call(
        kernel,
        in_specs=in_specs,
        out_specs=[VMEM] * len(outs),
        out_shape=[jax.ShapeDtypeStruct(shape, jnp.bfloat16) for shape in outs],
        scratch_shapes=scratch,
        cost_estimate=pl.CostEstimate(flops=0, bytes_accessed=0, transcendentals=0),
        compiler_params=pltpu.CompilerParams(vmem_limit_bytes=limit * 2**20),
    )(*ins)


def attention(spots, base, rows, allowed, pieces, qkv_width):
    length, width = rows.shape
    heads = qkv_width // (3 * HEAD_DIM)
    half = length // 2

    masks = [] if allowed is None else [allowed]

    def kernel(spots_ref, rows_ref, *refs):
        if allowed is None:
            seen = lax.broadcasted_iota(jnp.int32, (length, length), 0) >= lax.broadcasted_iota(
                jnp.int32, (length, length), 1
            )
        else:
            seen = refs[0][...] > 0
            refs = refs[1:]
        piece_refs = refs[: len(pieces)]
        keep, send, weight, projected, mixed, sems = refs[len(pieces) :]
        copies = load_weight(spots_ref, base, piece_refs, weight, sems)
        normed = norm(rows_ref[...].astype(jnp.float32))
        mixed[...] = jnp.zeros_like(mixed)
        for copy in copies:
            copy.wait()
        projected[...] = (
            jnp.dot(normed, weight[...], preferred_element_type=jnp.float32)
            .astype(jnp.bfloat16)
            .astype(jnp.float32)
        )
        for head in range(heads):
            at = head * 3 * HEAD_DIM
            query = projected[:, at : at + HEAD_DIM].astype(jnp.bfloat16)
            key = projected[:, at + HEAD_DIM : at + 2 * HEAD_DIM].astype(jnp.bfloat16)
            value = projected[:, at + 2 * HEAD_DIM : at + 3 * HEAD_DIM].astype(jnp.bfloat16)
            scores = dot_t(query, key) * HEAD_DIM ** (-0.5)
            scores = jnp.where(seen, scores, -1e30)
            exponent = jnp.exp(scores - jnp.max(scores, axis=-1, keepdims=True))
            soft = (exponent / jnp.sum(exponent, axis=-1, keepdims=True)).astype(jnp.bfloat16)
            out_at = qkv_width + head * HEAD_DIM
            mixed[:, out_at : out_at + HEAD_DIM] = jnp.dot(
                soft, value, preferred_element_type=jnp.float32
            )
        projected[...] = dot_t(mixed[...].astype(jnp.bfloat16), weight[...])
        core = spots_ref[24]
        keep[...] = projected[pl.ds(pl.multiple_of(core * half, 16), half), :].astype(jnp.bfloat16)
        send[...] = projected[pl.ds(pl.multiple_of((1 - core) * half, 16), half), :].astype(
            jnp.bfloat16
        )

    return local_call(
        kernel,
        [spots, rows] + masks + pieces,
        [SMEM, VMEM] + [VMEM] * len(masks) + [ANY] * len(pieces),
        [(half, width)] * 2,
        [
            pltpu.VMEM((width, width), jnp.bfloat16),
            pltpu.VMEM((length, width), jnp.float32),
            pltpu.VMEM((length, width), jnp.float32),
            pltpu.SemaphoreType.DMA((8,)),
        ],
    )


def middle(spots, rows, left, right):
    half, width = left.shape

    def kernel(spots_ref, rows_ref, left_ref, right_ref, mid, normed):
        base = rows_ref[pl.ds(pl.multiple_of(spots_ref[24] * half, 16), half), :]
        total = left_ref[...].astype(jnp.float32) + right_ref[...].astype(jnp.float32)
        value = (base.astype(jnp.float32) + total).astype(jnp.bfloat16)
        mid[...] = value
        normed[...] = norm(value.astype(jnp.float32))

    return local_call(
        kernel, [spots, rows, left, right], [SMEM, VMEM, VMEM, VMEM], [(half, width)] * 2, [], 16
    )


def feed_forward(spots, sources, weights, bases):
    half, width = sources[0].shape
    units = width // 2
    pieces = [piece for weight in weights for piece in weight]
    parts = len(weights)
    rows = len(sources)

    def kernel(spots_ref, *refs):
        source_refs, piece_refs, refs = (
            refs[:rows],
            refs[rows : rows + len(pieces)],
            refs[rows + len(pieces) :],
        )
        targets, scratch = refs[:rows], refs[rows:]
        copies, at = [], 0
        for part in range(parts):
            mine = piece_refs[at : at + len(weights[part])]
            at += len(mine)
            copies += load_weight(spots_ref, bases[part], mine, scratch[part], scratch[parts + part])
        for copy in copies:
            copy.wait()
        if parts == 1:
            up, down = scratch[0][:, :units], scratch[0][:, units:]
        else:
            up, down = scratch[0][...], scratch[1][...]
        for source, target in zip(source_refs, targets):
            hidden = jnp.dot(source[...], up, preferred_element_type=jnp.float32)
            hidden = 0.5 * hidden * (1.0 + lax.erf(hidden * 0.5**0.5))
            target[...] = dot_t(hidden.astype(jnp.bfloat16), down).astype(jnp.bfloat16)

    return local_call(
        kernel,
        [spots] + sources + pieces,
        [SMEM] + [VMEM] * rows + [ANY] * len(pieces),
        [(half, width)] * rows,
        [pltpu.VMEM((width, weight[0].shape[1]), jnp.bfloat16) for weight in weights]
        + [pltpu.SemaphoreType.DMA((8,))] * parts,
    )


def merge(spots, base, blocks, pieces):
    count, width = blocks.shape
    half = width // 2

    def kernel(spots_ref, blocks_ref, *refs):
        piece_refs = refs[: len(pieces)]
        keep, send, weight, sems = refs[len(pieces) :]
        for copy in load_weight(spots_ref, base, piece_refs, weight, sems):
            copy.wait()
        core = spots_ref[24]
        source = blocks_ref[...]
        for side, target in ((core, keep), (1 - core, send)):
            rows = weight[pl.ds(pl.multiple_of(side * half, 16), half), :]
            target[...] = dot_t(source, rows).astype(jnp.bfloat16)

    return local_call(
        kernel,
        [spots, blocks] + pieces,
        [SMEM, VMEM] + [ANY] * len(pieces),
        [(count, half)] * 2,
        [pltpu.VMEM((width, width), jnp.bfloat16), pltpu.SemaphoreType.DMA((8,))],
    )


def pick(rows, which, axis):
    return lax.dynamic_index_in_dim(rows, which, axis, keepdims=False)


def add_short(left, right):
    return left.astype(jnp.float32) + right.astype(jnp.float32)


def join_core(half, axis):
    _, _, _, c = place()
    other = swap_core(half)
    first = jnp.where(c == 0, half, other)
    second = jnp.where(c == 0, other, half)
    return jnp.concatenate([first, second], axis=axis)


def exchange_y(blocks):
    _, y, _, _ = place()
    groups = blocks.shape[1]
    if groups > 1:
        members = [[i * groups + g for g in range(groups)] for i in range(8)]
        blocks = lax.all_to_all(
            blocks, "req", split_axis=1, concat_axis=1, tiled=True, axis_index_groups=members
        )
    blocks = blocks.reshape((4, 2) + blocks.shape[1:])
    return jnp.stack([pick(blocks, y, 1), swap_y(pick(blocks, 1 - y, 1))], axis=1)


def exchange_z(both):
    z, _, _, _ = place()
    mixed = [pick(both, z, 0)] + [swap_z(pick(both, z ^ k, 0), k) for k in (1, 2, 3)]
    return jnp.concatenate(mixed, axis=0)


def on_device(
    patches,
    half_grid,
    text_embed,
    dest_dev,
    dest_pos,
    text_len,
    enc_qkv,
    enc_out_t,
    enc_up,
    enc_down_t,
    merge_t,
    dec_qkv,
    dec_out_t,
    dec_up,
    dec_down_t,
):
    _, _, x, c = place()
    senders = lax.axis_size("req")
    image_count = half_grid.shape[0]
    model_width = patches.shape[1]
    cells = HALF * HALF
    slot_count = image_count * cells
    qkv_width = enc_qkv.shape[1]
    half_width = model_width // 2
    spots = block_places()

    enc_attn = own_rows(jnp.concatenate([enc_qkv, enc_out_t], axis=1))
    enc_up, enc_down_t = own_rows(enc_up), own_rows(enc_down_t)
    merge_t = own_rows(merge_t)
    dec_attn = own_rows(jnp.concatenate([dec_qkv, dec_out_t], axis=1))
    dec_up, dec_down_t = own_rows(dec_up), own_rows(dec_down_t)

    first, second, y_own = swap_z(enc_attn, 1), swap_z(enc_attn, 2), swap_y(enc_attn)
    first, second, y_own, enc_up, enc_down_t = together(first, second, y_own, enc_up, enc_down_t)
    third = swap_z(second, 1)
    y_early = swap_y(jnp.concatenate([first, second], axis=0))

    up, down = halves_by_z(enc_up), halves_by_z(enc_down_t)
    mine, others = [jnp.concatenate(pair, axis=1) for pair in zip(up, down)]
    third, near = together(third, others)
    enc_ff = Halved(mine, others, near)
    enc_attn = [enc_attn, first, second, third, y_own, y_early, swap_y(third)]
    enc_ff.third, merge_t = together(enc_ff.third, merge_t)
    enc_ff = enc_ff.pieces()

    merge_second = swap_z(merge_t, 2)

    cell_index = jnp.arange(cells, dtype=jnp.int32)
    slot_valid = ((cell_index // HALF)[None, :] < half_grid[:, 0:1]) & (
        (cell_index % HALF)[None, :] < half_grid[:, 1:2]
    )
    slot_valid = slot_valid.reshape(-1)

    rows = patches.reshape(image_count, HALF, 2, HALF, 2, model_width)
    rows = rows.transpose(4, 2, 0, 1, 3, 5).reshape(4 * slot_count, model_width)
    image_of = jnp.tile(jnp.arange(slot_count, dtype=jnp.int32) // cells, 4)
    allowed = (image_of[:, None] == image_of[None, :]) & jnp.tile(slot_valid, 4)[None, :]
    allowed = allowed.astype(jnp.float32)

    keep, send = attention(spots, DIRECT, rows, allowed, enc_attn, qkv_width)
    mine = add_short(keep, swap_core(send)).astype(jnp.bfloat16)
    mid, normed = middle(spots, rows, mine, swap_x(mine))
    normed, merge_second = together(normed, merge_second)
    normed_pair = swap_z(normed, 1)
    sources = [normed, swap_core(normed), normed_pair, swap_core(normed_pair)]
    merge_two = jnp.concatenate([merge_t, merge_second], axis=0)
    merge_pair = swap_z(merge_two, 1)
    merge_two_y = swap_y(merge_two)
    own_keep, own_send, pair_keep, pair_send = feed_forward(spots, sources, [enc_ff], [DIRECT])
    pair_sum = add_short(pair_keep, swap_core(pair_send)).astype(jnp.bfloat16)
    pair_sum, merge_pair, merge_two_y, dec_attn = together(
        pair_sum, merge_pair, merge_two_y, dec_attn
    )
    arrived = swap_z(pair_sum, 1)
    attn_second = swap_z(dec_attn, 2)
    merge_all = [merge_two, merge_two_y, merge_pair, swap_y(merge_pair)]
    own_sum = add_short(own_keep, swap_core(own_send))
    total = (own_sum + arrived.astype(jnp.float32)).astype(jnp.bfloat16)
    total = total.reshape(2, slot_count, model_width)
    total = add_short(pick(total, x, 0), swap_x(pick(total, 1 - x, 0)))
    kept = pick(mid.reshape(2, slot_count, model_width), x, 0)
    encoded = (kept.astype(jnp.float32) + total).astype(jnp.bfloat16)

    encoded, attn_second = together(encoded, attn_second)
    attn_two = jnp.concatenate([dec_attn, attn_second], axis=0)
    attn_pair = swap_z(attn_two, 1)
    attn_two_y = swap_y(attn_two)
    keep, send = merge(spots, WHOLE, encoded, merge_all)
    merged = add_short(keep, swap_core(send))
    merged = merged.astype(jnp.bfloat16)
    merged = add_short(merged, swap_x(merged)).astype(jnp.bfloat16)

    even_share = slot_count // senders
    capacity = even_share + max(even_share // 2, 1)
    padded = -(-capacity // 16) * 16
    one_hot = (dest_dev[:, None] == jnp.arange(senders, dtype=jnp.int32)[None, :]).astype(jnp.int32)
    earlier = jnp.cumsum(one_hot, axis=0) - one_hot
    slot_rank = jnp.sum(earlier * one_hot, axis=1)
    bucket = dest_dev * padded + slot_rank
    chosen = jnp.arange(senders * padded, dtype=jnp.int32)[:, None] == bucket[None, :]
    digits = jnp.stack([slot_valid.astype(jnp.int32), dest_pos // 128, dest_pos % 128], 1)
    digits = jnp.pad(digits, ((0, 0), (0, 125))).astype(jnp.bfloat16)
    outgoing = jnp.dot(
        chosen.astype(jnp.bfloat16),
        jnp.concatenate([merged, digits], axis=1),
        preferred_element_type=jnp.float32,
    ).astype(jnp.bfloat16)
    outgoing, attn_pair, attn_two_y, dec_up = together(outgoing, attn_pair, attn_two_y, dec_up)
    mine, others = halves_by_z(dec_up)
    dec_up = Halved(mine, others, others)
    both = exchange_y(outgoing.reshape(8, senders // 8, padded, -1))
    both, attn_pair = together(both, attn_pair)
    dec_up = dec_up.pieces()
    attn_pair_y = swap_y(attn_pair)
    incoming = exchange_z(both)
    incoming, attn_pair_y, dec_down_t = together(incoming, attn_pair_y, dec_down_t)
    dec_attn = [attn_two, attn_two_y, attn_pair, attn_pair_y]
    dec_down = halved_column(dec_down_t)
    incoming = incoming.reshape(senders * padded, -1)

    seq_len = text_embed.shape[0]
    half_rows = seq_len // 2
    positions = jnp.arange(seq_len, dtype=jnp.int32)
    marks = incoming[:, half_width:].astype(jnp.int32)
    target = jnp.where(marks[:, 0] > 0, marks[:, 1] * 128 + marks[:, 2], -1)
    hits = positions[:, None] == target[None, :]
    placed = jnp.dot(
        hits.astype(jnp.bfloat16), incoming[:, :half_width], preferred_element_type=jnp.float32
    ).astype(jnp.bfloat16)
    text_half = lax.dynamic_slice_in_dim(text_embed, c * half_width, half_width, 1)
    dec_half = jnp.where(jnp.any(hits, axis=1)[:, None], placed, text_half)
    rows = join_core(dec_half, 1)
    causal = None
    keep, send = attention(spots, WHOLE, rows, causal, dec_attn, qkv_width)
    send, *dec_up = together(send, *dec_up)
    mine = add_short(keep, swap_core(send)).astype(jnp.bfloat16)
    mid, normed = middle(spots, rows, mine, swap_x(mine))
    normed_pair = swap_z(normed, 1)
    sources = [normed, swap_core(normed), normed_pair, swap_core(normed_pair)]
    own_keep, own_send, pair_keep, pair_send = feed_forward(spots, sources, [dec_up, dec_down], [DIRECT, COLUMNS])
    pair_sum = add_short(pair_keep, swap_core(pair_send)).astype(jnp.bfloat16)
    arrived = swap_z(pair_sum, 1)
    own_sum = add_short(own_keep, swap_core(own_send))
    total = (own_sum + arrived.astype(jnp.float32)).astype(jnp.bfloat16)
    total = add_short(total, swap_x(total))
    decoded = (mid.astype(jnp.float32) + total).astype(jnp.bfloat16)
    keep_mask = positions < slot_count + text_len[0]
    keep_half = pick(keep_mask.reshape(2, half_rows), c, 0)
    decoded = jnp.where(keep_half[:, None], decoded, jnp.zeros_like(decoded))
    return join_core(decoded, 0)


def solution(mesh):
    return jax.shard_map(
        on_device,
        mesh=mesh,
        in_specs=(
            P("req", None),
            P("req", None),
            P("req", None),
            P("req"),
            P("req"),
            P("req"),
            P("req", "tp"),
            P("req", "tp"),
            P("req", "tp"),
            P("req", "tp"),
            P("req", "tp"),
            P("req", "tp"),
            P("req", "tp"),
            P("req", "tp"),
            P("req", "tp"),
        ),
        out_specs=P("req", None),
        check_vma=False,
    )
```

```python
import jax
import jax.numpy as jnp
from jax import lax
from jax.experimental import pallas as pl
from jax.experimental.pallas import tpu as pltpu
from jax.sharding import PartitionSpec as P

HEAD_DIM = 80
GRID = 16
HALF = GRID // 2
EPS = 1e-06
AXES = ("req", "tp")


def routes(move):
    groups = lax.axis_size("req") // 8
    pairs = []
    for z in range(4):
        for y in range(2):
            for x in range(2):
                for c in range(2):
                    z2, y2, x2, c2 = move(z, y, x, c)
                    for g in range(groups):
                        source = ((z * 2 + y) * groups + g) * 4 + x * 2 + c
                        target = ((z2 * 2 + y2) * groups + g) * 4 + x2 * 2 + c2
                        pairs.append((source, target))
    return pairs


def swap_core(part):
    return lax.ppermute(part, AXES, routes(lambda z, y, x, c: (z, y, x, 1 - c)))


def swap_x(part):
    return lax.ppermute(part, AXES, routes(lambda z, y, x, c: (z, y, 1 - x, c)))


def swap_y(part):
    return lax.ppermute(part, AXES, routes(lambda z, y, x, c: (z, 1 - y, x, c)))


def swap_z(part, k):
    return lax.ppermute(part, AXES, routes(lambda z, y, x, c: (z ^ k, y, x, c)))


def place():
    index = lax.axis_index("req") // (lax.axis_size("req") // 8)
    tensor = lax.axis_index("tp")
    return index // 2, index % 2, tensor // 2, tensor % 2


def own_rows(weight):
    groups = lax.axis_size("req") // 8
    if groups == 1:
        return weight
    members = [[i * groups + g for g in range(groups)] for i in range(8)]
    return lax.all_gather(weight, "req", axis=0, tiled=True, axis_index_groups=members)


def together(*values):
    return lax.optimization_barrier(values)


def halves_by_z(weight):
    z, _, _, _ = place()
    half = weight.shape[1] // 2
    return [
        lax.dynamic_slice_in_dim(weight, ((z % 2) ^ bit) * half, half, 1) for bit in (0, 1)
    ]


class Halved:
    def __init__(self, mine, others, near):
        self.own = mine
        self.first = swap_z(near, 1)
        self.second = swap_z(mine, 2)
        self.third = swap_z(others, 3)
        self.y_own = swap_y(mine)

    def pieces(self):
        column = jnp.concatenate([self.first, self.second, self.third], axis=0)
        column, self.y_own = together(column, self.y_own)
        return [self.own, column, self.y_own, swap_y(column)]


def halved_column(weight):
    groups = lax.axis_size("req") // 8
    half = weight.shape[1] // 2
    members = [
        [(z * 2 + y) * groups + g for z in range(4)] for y in range(2) for g in range(groups)
    ]
    column = lax.all_to_all(
        jnp.stack([weight[:, :half], weight[:, half:]] * 2),
        "req",
        split_axis=0,
        concat_axis=0,
        tiled=True,
        axis_index_groups=members,
    ).reshape(-1, half)
    return [column, swap_y(column)]


def block_places():
    z, y, _, c = place()
    direct = [(z ^ k) * 2 + (y ^ v) for v in range(2) for k in range(4)]
    whole = [(z ^ k) * 2 + (y ^ v) for ks in ((0, 2), (1, 3)) for v in range(2) for k in ks]
    columns = [k * 2 + (y ^ v) for v in range(2) for k in range(4)]
    return jnp.stack(direct + whole + columns + [c]).astype(jnp.int32)


def load_weight(spots, base, pieces, weight, sems):
    height = weight.shape[0] // 8
    copies = []
    for piece in pieces:
        for block in range(piece.shape[0] // height):
            at = len(copies)
            start = pl.multiple_of(spots[base + at] * height, 16)
            copies.append(
                pltpu.make_async_copy(
                    piece.at[pl.ds(block * height, height)],
                    weight.at[pl.ds(start, height)],
                    sems.at[at],
                )
            )
    for copy in copies:
        copy.start()
    return copies


def norm(values_f):
    center = values_f - jnp.mean(values_f, axis=-1, keepdims=True)
    spread = jnp.mean(center * center, axis=-1, keepdims=True)
    return (center * lax.rsqrt(spread + EPS)).astype(jnp.bfloat16)


def dot_t(left, right):
    return lax.dot_general(left, right, (((1,), (1,)), ((), ())), preferred_element_type=jnp.float32)


DIRECT, WHOLE, COLUMNS = 0, 8, 16
VMEM = pl.BlockSpec(memory_space=pltpu.VMEM)
SMEM = pl.BlockSpec(memory_space=pltpu.SMEM)
ANY = pl.BlockSpec(memory_space=pl.ANY)


def local_call(kernel, ins, in_specs, outs, scratch, limit=28):
    return pl.pallas_call(
        kernel,
        in_specs=in_specs,
        out_specs=[VMEM] * len(outs),
        out_shape=[jax.ShapeDtypeStruct(shape, jnp.bfloat16) for shape in outs],
        scratch_shapes=scratch,
        cost_estimate=pl.CostEstimate(flops=0, bytes_accessed=0, transcendentals=0),
        compiler_params=pltpu.CompilerParams(vmem_limit_bytes=limit * 2**20),
    )(*ins)


def attention(spots, base, rows, allowed, pieces, qkv_width):
    length, width = rows.shape
    heads = qkv_width // (3 * HEAD_DIM)
    half = length // 2

    masks = [] if allowed is None else [allowed]

    def kernel(spots_ref, rows_ref, *refs):
        if allowed is None:
            seen = lax.broadcasted_iota(jnp.int32, (length, length), 0) >= lax.broadcasted_iota(
                jnp.int32, (length, length), 1
            )
        else:
            seen = refs[0][...] > 0
            refs = refs[1:]
        piece_refs = refs[: len(pieces)]
        keep, send, weight, projected, mixed, sems = refs[len(pieces) :]
        copies = load_weight(spots_ref, base, piece_refs, weight, sems)
        normed = norm(rows_ref[...].astype(jnp.float32))
        mixed[...] = jnp.zeros_like(mixed)
        for copy in copies:
            copy.wait()
        projected[...] = (
            jnp.dot(normed, weight[...], preferred_element_type=jnp.float32)
            .astype(jnp.bfloat16)
            .astype(jnp.float32)
        )
        for head in range(heads):
            at = head * 3 * HEAD_DIM
            query = projected[:, at : at + HEAD_DIM].astype(jnp.bfloat16)
            key = projected[:, at + HEAD_DIM : at + 2 * HEAD_DIM].astype(jnp.bfloat16)
            value = projected[:, at + 2 * HEAD_DIM : at + 3 * HEAD_DIM].astype(jnp.bfloat16)
            scores = dot_t(query, key) * HEAD_DIM ** (-0.5)
            scores = jnp.where(seen, scores, -1e30)
            exponent = jnp.exp(scores - jnp.max(scores, axis=-1, keepdims=True))
            soft = (exponent / jnp.sum(exponent, axis=-1, keepdims=True)).astype(jnp.bfloat16)
            out_at = qkv_width + head * HEAD_DIM
            mixed[:, out_at : out_at + HEAD_DIM] = jnp.dot(
                soft, value, preferred_element_type=jnp.float32
            )
        projected[...] = dot_t(mixed[...].astype(jnp.bfloat16), weight[...])
        core = spots_ref[24]
        keep[...] = projected[pl.ds(pl.multiple_of(core * half, 16), half), :].astype(jnp.bfloat16)
        send[...] = projected[pl.ds(pl.multiple_of((1 - core) * half, 16), half), :].astype(
            jnp.bfloat16
        )

    return local_call(
        kernel,
        [spots, rows] + masks + pieces,
        [SMEM, VMEM] + [VMEM] * len(masks) + [ANY] * len(pieces),
        [(half, width)] * 2,
        [
            pltpu.VMEM((width, width), jnp.bfloat16),
            pltpu.VMEM((length, width), jnp.float32),
            pltpu.VMEM((length, width), jnp.float32),
            pltpu.SemaphoreType.DMA((8,)),
        ],
    )


def middle(spots, rows, left, right):
    half, width = left.shape

    def kernel(spots_ref, rows_ref, left_ref, right_ref, mid, normed):
        base = rows_ref[pl.ds(pl.multiple_of(spots_ref[24] * half, 16), half), :]
        total = left_ref[...].astype(jnp.float32) + right_ref[...].astype(jnp.float32)
        value = (base.astype(jnp.float32) + total).astype(jnp.bfloat16)
        mid[...] = value
        normed[...] = norm(value.astype(jnp.float32))

    return local_call(
        kernel, [spots, rows, left, right], [SMEM, VMEM, VMEM, VMEM], [(half, width)] * 2, [], 16
    )


def feed_forward(spots, sources, weights, bases):
    half, width = sources[0].shape
    units = width // 2
    pieces = [piece for weight in weights for piece in weight]
    parts = len(weights)
    rows = len(sources)

    def kernel(spots_ref, *refs):
        source_refs, piece_refs, refs = (
            refs[:rows],
            refs[rows : rows + len(pieces)],
            refs[rows + len(pieces) :],
        )
        targets, scratch = refs[:rows], refs[rows:]
        copies, at = [], 0
        for part in range(parts):
            mine = piece_refs[at : at + len(weights[part])]
            at += len(mine)
            copies += load_weight(spots_ref, bases[part], mine, scratch[part], scratch[parts + part])
        for copy in copies:
            copy.wait()
        if parts == 1:
            up, down = scratch[0][:, :units], scratch[0][:, units:]
        else:
            up, down = scratch[0][...], scratch[1][...]
        hidden = jnp.concatenate([source[...] for source in source_refs], axis=0)
        hidden = jnp.dot(hidden, up, preferred_element_type=jnp.float32)
        hidden = 0.5 * hidden * (1.0 + lax.erf(hidden * 0.5**0.5))
        result = dot_t(hidden.astype(jnp.bfloat16), down).astype(jnp.bfloat16)
        for at, target in enumerate(targets):
            target[...] = result[at * half : (at + 1) * half]

    return local_call(
        kernel,
        [spots] + sources + pieces,
        [SMEM] + [VMEM] * rows + [ANY] * len(pieces),
        [(half, width)] * rows,
        [pltpu.VMEM((width, weight[0].shape[1]), jnp.bfloat16) for weight in weights]
        + [pltpu.SemaphoreType.DMA((8,))] * parts,
    )


def merge(spots, base, blocks, pieces):
    count, width = blocks.shape
    half = width // 2

    def kernel(spots_ref, blocks_ref, *refs):
        piece_refs = refs[: len(pieces)]
        keep, send, weight, sems = refs[len(pieces) :]
        for copy in load_weight(spots_ref, base, piece_refs, weight, sems):
            copy.wait()
        core = spots_ref[24]
        source = blocks_ref[...]
        for side, target in ((core, keep), (1 - core, send)):
            rows = weight[pl.ds(pl.multiple_of(side * half, 16), half), :]
            target[...] = dot_t(source, rows).astype(jnp.bfloat16)

    return local_call(
        kernel,
        [spots, blocks] + pieces,
        [SMEM, VMEM] + [ANY] * len(pieces),
        [(count, half)] * 2,
        [pltpu.VMEM((width, width), jnp.bfloat16), pltpu.SemaphoreType.DMA((8,))],
    )


def pick(rows, which, axis):
    return lax.dynamic_index_in_dim(rows, which, axis, keepdims=False)


def add_short(left, right):
    return left.astype(jnp.float32) + right.astype(jnp.float32)


def join_core(half, axis):
    _, _, _, c = place()
    other = swap_core(half)
    first = jnp.where(c == 0, half, other)
    second = jnp.where(c == 0, other, half)
    return jnp.concatenate([first, second], axis=axis)


def exchange_y(blocks):
    _, y, _, _ = place()
    groups = blocks.shape[1]
    if groups > 1:
        members = [[i * groups + g for g in range(groups)] for i in range(8)]
        blocks = lax.all_to_all(
            blocks, "req", split_axis=1, concat_axis=1, tiled=True, axis_index_groups=members
        )
    blocks = blocks.reshape((4, 2) + blocks.shape[1:])
    return jnp.stack([pick(blocks, y, 1), swap_y(pick(blocks, 1 - y, 1))], axis=1)


def exchange_z(both):
    z, _, _, _ = place()
    mixed = [pick(both, z, 0)] + [swap_z(pick(both, z ^ k, 0), k) for k in (1, 2, 3)]
    return jnp.concatenate(mixed, axis=0)


def on_device(
    patches,
    half_grid,
    text_embed,
    dest_dev,
    dest_pos,
    text_len,
    enc_qkv,
    enc_out_t,
    enc_up,
    enc_down_t,
    merge_t,
    dec_qkv,
    dec_out_t,
    dec_up,
    dec_down_t,
):
    _, _, x, c = place()
    senders = lax.axis_size("req")
    image_count = half_grid.shape[0]
    model_width = patches.shape[1]
    cells = HALF * HALF
    slot_count = image_count * cells
    qkv_width = enc_qkv.shape[1]
    half_width = model_width // 2
    spots = block_places()

    enc_attn = own_rows(jnp.concatenate([enc_qkv, enc_out_t], axis=1))
    enc_up, enc_down_t = own_rows(enc_up), own_rows(enc_down_t)
    merge_t = own_rows(merge_t)
    dec_attn = own_rows(jnp.concatenate([dec_qkv, dec_out_t], axis=1))
    dec_up, dec_down_t = own_rows(dec_up), own_rows(dec_down_t)

    first, second, y_own = swap_z(enc_attn, 1), swap_z(enc_attn, 2), swap_y(enc_attn)
    first, second, y_own, enc_up, enc_down_t = together(first, second, y_own, enc_up, enc_down_t)
    third = swap_z(second, 1)
    y_early = swap_y(jnp.concatenate([first, second], axis=0))

    up, down = halves_by_z(enc_up), halves_by_z(enc_down_t)
    mine, others = [jnp.concatenate(pair, axis=1) for pair in zip(up, down)]
    third, near = together(third, others)
    enc_ff = Halved(mine, others, near)
    enc_attn = [enc_attn, first, second, third, y_own, y_early, swap_y(third)]
    enc_ff.third, merge_t = together(enc_ff.third, merge_t)
    enc_ff = enc_ff.pieces()

    merge_second = swap_z(merge_t, 2)

    cell_index = jnp.arange(cells, dtype=jnp.int32)
    slot_valid = ((cell_index // HALF)[None, :] < half_grid[:, 0:1]) & (
        (cell_index % HALF)[None, :] < half_grid[:, 1:2]
    )
    slot_valid = slot_valid.reshape(-1)

    rows = patches.reshape(image_count, HALF, 2, HALF, 2, model_width)
    rows = rows.transpose(4, 2, 0, 1, 3, 5).reshape(4 * slot_count, model_width)
    image_of = jnp.tile(jnp.arange(slot_count, dtype=jnp.int32) // cells, 4)
    allowed = (image_of[:, None] == image_of[None, :]) & jnp.tile(slot_valid, 4)[None, :]
    allowed = allowed.astype(jnp.float32)

    keep, send = attention(spots, DIRECT, rows, allowed, enc_attn, qkv_width)
    mine = add_short(keep, swap_core(send)).astype(jnp.bfloat16)
    mid, normed = middle(spots, rows, mine, swap_x(mine))
    normed_pair = swap_z(normed, 1)
    normed_pair, merge_second = together(normed_pair, merge_second)
    sources = [normed, swap_core(normed), normed_pair, swap_core(normed_pair)]
    merge_two = jnp.concatenate([merge_t, merge_second], axis=0)
    merge_pair = swap_z(merge_two, 1)
    merge_two_y = swap_y(merge_two)
    own_keep, own_send, pair_keep, pair_send = feed_forward(spots, sources, [enc_ff], [DIRECT])
    pair_sum = add_short(pair_keep, swap_core(pair_send)).astype(jnp.bfloat16)
    pair_sum, merge_pair, merge_two_y, dec_attn = together(
        pair_sum, merge_pair, merge_two_y, dec_attn
    )
    arrived = swap_z(pair_sum, 1)
    attn_second = swap_z(dec_attn, 2)
    merge_all = [merge_two, merge_two_y, merge_pair, swap_y(merge_pair)]
    own_sum = add_short(own_keep, swap_core(own_send))
    total = (own_sum + arrived.astype(jnp.float32)).astype(jnp.bfloat16)
    total = total.reshape(2, slot_count, model_width)
    total = add_short(pick(total, x, 0), swap_x(pick(total, 1 - x, 0)))
    kept = pick(mid.reshape(2, slot_count, model_width), x, 0)
    encoded = (kept.astype(jnp.float32) + total).astype(jnp.bfloat16)

    encoded, attn_second = together(encoded, attn_second)
    attn_two = jnp.concatenate([dec_attn, attn_second], axis=0)
    attn_pair = swap_z(attn_two, 1)
    attn_two_y = swap_y(attn_two)
    keep, send = merge(spots, WHOLE, encoded, merge_all)
    merged = add_short(keep, swap_core(send))
    merged = merged.astype(jnp.bfloat16)
    merged = add_short(merged, swap_x(merged)).astype(jnp.bfloat16)

    even_share = slot_count // senders
    capacity = even_share + max(even_share // 2, 1)
    padded = -(-capacity // 16) * 16
    one_hot = (dest_dev[:, None] == jnp.arange(senders, dtype=jnp.int32)[None, :]).astype(jnp.int32)
    earlier = jnp.cumsum(one_hot, axis=0) - one_hot
    slot_rank = jnp.sum(earlier * one_hot, axis=1)
    bucket = dest_dev * padded + slot_rank
    chosen = jnp.arange(senders * padded, dtype=jnp.int32)[:, None] == bucket[None, :]
    digits = jnp.stack([slot_valid.astype(jnp.int32), dest_pos // 128, dest_pos % 128], 1)
    digits = jnp.pad(digits, ((0, 0), (0, 125))).astype(jnp.bfloat16)
    outgoing = jnp.dot(
        chosen.astype(jnp.bfloat16),
        jnp.concatenate([merged, digits], axis=1),
        preferred_element_type=jnp.float32,
    ).astype(jnp.bfloat16)
    outgoing, attn_pair, attn_two_y, dec_up = together(outgoing, attn_pair, attn_two_y, dec_up)
    mine, others = halves_by_z(dec_up)
    dec_up = Halved(mine, others, others)
    both = exchange_y(outgoing.reshape(8, senders // 8, padded, -1))
    both, attn_pair = together(both, attn_pair)
    dec_up = dec_up.pieces()
    attn_pair_y = swap_y(attn_pair)
    incoming = exchange_z(both)
    incoming, attn_pair_y, dec_down_t = together(incoming, attn_pair_y, dec_down_t)
    dec_attn = [attn_two, attn_two_y, attn_pair, attn_pair_y]
    dec_down = halved_column(dec_down_t)
    incoming = incoming.reshape(senders * padded, -1)

    seq_len = text_embed.shape[0]
    half_rows = seq_len // 2
    positions = jnp.arange(seq_len, dtype=jnp.int32)
    marks = incoming[:, half_width:].astype(jnp.int32)
    target = jnp.where(marks[:, 0] > 0, marks[:, 1] * 128 + marks[:, 2], -1)
    hits = positions[:, None] == target[None, :]
    placed = jnp.dot(
        hits.astype(jnp.bfloat16), incoming[:, :half_width], preferred_element_type=jnp.float32
    ).astype(jnp.bfloat16)
    text_half = lax.dynamic_slice_in_dim(text_embed, c * half_width, half_width, 1)
    dec_half = jnp.where(jnp.any(hits, axis=1)[:, None], placed, text_half)
    rows = join_core(dec_half, 1)
    causal = None
    keep, send = attention(spots, WHOLE, rows, causal, dec_attn, qkv_width)
    send, *dec_up = together(send, *dec_up)
    mine = add_short(keep, swap_core(send)).astype(jnp.bfloat16)
    mid, normed = middle(spots, rows, mine, swap_x(mine))
    normed_pair = swap_z(normed, 1)
    sources = [normed, swap_core(normed), normed_pair, swap_core(normed_pair)]
    own_keep, own_send, pair_keep, pair_send = feed_forward(spots, sources, [dec_up, dec_down], [DIRECT, COLUMNS])
    pair_sum = add_short(pair_keep, swap_core(pair_send)).astype(jnp.bfloat16)
    arrived = swap_z(pair_sum, 1)
    own_sum = add_short(own_keep, swap_core(own_send))
    total = (own_sum + arrived.astype(jnp.float32)).astype(jnp.bfloat16)
    total = add_short(total, swap_x(total))
    decoded = (mid.astype(jnp.float32) + total).astype(jnp.bfloat16)
    keep_mask = positions < slot_count + text_len[0]
    keep_half = pick(keep_mask.reshape(2, half_rows), c, 0)
    decoded = jnp.where(keep_half[:, None], decoded, jnp.zeros_like(decoded))
    return join_core(decoded, 0)


def solution(mesh):
    return jax.shard_map(
        on_device,
        mesh=mesh,
        in_specs=(
            P("req", None),
            P("req", None),
            P("req", None),
            P("req"),
            P("req"),
            P("req"),
            P("req", "tp"),
            P("req", "tp"),
            P("req", "tp"),
            P("req", "tp"),
            P("req", "tp"),
            P("req", "tp"),
            P("req", "tp"),
            P("req", "tp"),
            P("req", "tp"),
        ),
        out_specs=P("req", None),
        check_vma=False,
    )
```

```python
import jax
import jax.numpy as jnp
from jax import lax
from jax.experimental import pallas as pl
from jax.experimental.pallas import tpu as pltpu
from jax.sharding import PartitionSpec as P

HEAD_DIM = 80
GRID = 16
HALF = GRID // 2
EPS = 1e-06
AXES = ("req", "tp")


def routes(move):
    groups = lax.axis_size("req") // 8
    pairs = []
    for z in range(4):
        for y in range(2):
            for x in range(2):
                for c in range(2):
                    z2, y2, x2, c2 = move(z, y, x, c)
                    for g in range(groups):
                        source = ((z * 2 + y) * groups + g) * 4 + x * 2 + c
                        target = ((z2 * 2 + y2) * groups + g) * 4 + x2 * 2 + c2
                        pairs.append((source, target))
    return pairs


def swap_core(part):
    return lax.ppermute(part, AXES, routes(lambda z, y, x, c: (z, y, x, 1 - c)))


def swap_x(part):
    return lax.ppermute(part, AXES, routes(lambda z, y, x, c: (z, y, 1 - x, c)))


def swap_y(part):
    return lax.ppermute(part, AXES, routes(lambda z, y, x, c: (z, 1 - y, x, c)))


def swap_z(part, k):
    return lax.ppermute(part, AXES, routes(lambda z, y, x, c: (z ^ k, y, x, c)))


def place():
    index = lax.axis_index("req") // (lax.axis_size("req") // 8)
    tensor = lax.axis_index("tp")
    return index // 2, index % 2, tensor // 2, tensor % 2


def own_rows(weight):
    groups = lax.axis_size("req") // 8
    if groups == 1:
        return weight
    members = [[i * groups + g for g in range(groups)] for i in range(8)]
    return lax.all_gather(weight, "req", axis=0, tiled=True, axis_index_groups=members)


def together(*values):
    return lax.optimization_barrier(values)


def halves_by_z(weight):
    z, _, _, _ = place()
    half = weight.shape[1] // 2
    return [
        lax.dynamic_slice_in_dim(weight, ((z % 2) ^ bit) * half, half, 1) for bit in (0, 1)
    ]


class Halved:
    def __init__(self, mine, others, near):
        self.own = mine
        self.first = swap_z(near, 1)
        self.second = swap_z(mine, 2)
        self.third = swap_z(others, 3)
        self.y_own = swap_y(mine)

    def pieces(self):
        column = jnp.concatenate([self.first, self.second, self.third], axis=0)
        column, self.y_own = together(column, self.y_own)
        return [self.own, column, self.y_own, swap_y(column)]


def halved_column(weight):
    groups = lax.axis_size("req") // 8
    half = weight.shape[1] // 2
    members = [
        [(z * 2 + y) * groups + g for z in range(4)] for y in range(2) for g in range(groups)
    ]
    column = lax.all_to_all(
        jnp.stack([weight[:, :half], weight[:, half:]] * 2),
        "req",
        split_axis=0,
        concat_axis=0,
        tiled=True,
        axis_index_groups=members,
    ).reshape(-1, half)
    return [column, swap_y(column)]


def block_places():
    z, y, _, c = place()
    direct = [(z ^ k) * 2 + (y ^ v) for v in range(2) for k in range(4)]
    whole = [(z ^ k) * 2 + (y ^ v) for ks in ((0, 2), (1, 3)) for v in range(2) for k in ks]
    columns = [k * 2 + (y ^ v) for v in range(2) for k in range(4)]
    return jnp.stack(direct + whole + columns + [c]).astype(jnp.int32)


def load_weight(spots, base, pieces, weight, sems):
    height = weight.shape[0] // 8
    copies = []
    for piece in pieces:
        for block in range(piece.shape[0] // height):
            at = len(copies)
            start = pl.multiple_of(spots[base + at] * height, 16)
            copies.append(
                pltpu.make_async_copy(
                    piece.at[pl.ds(block * height, height)],
                    weight.at[pl.ds(start, height)],
                    sems.at[at],
                )
            )
    for copy in copies:
        copy.start()
    return copies


def norm(values_f):
    center = values_f - jnp.mean(values_f, axis=-1, keepdims=True)
    spread = jnp.mean(center * center, axis=-1, keepdims=True)
    return (center * lax.rsqrt(spread + EPS)).astype(jnp.bfloat16)


def dot_t(left, right):
    return lax.dot_general(left, right, (((1,), (1,)), ((), ())), preferred_element_type=jnp.float32)


DIRECT, WHOLE, COLUMNS = 0, 8, 16
VMEM = pl.BlockSpec(memory_space=pltpu.VMEM)
SMEM = pl.BlockSpec(memory_space=pltpu.SMEM)
ANY = pl.BlockSpec(memory_space=pl.ANY)


def local_call(kernel, ins, in_specs, outs, scratch, limit=28):
    return pl.pallas_call(
        kernel,
        in_specs=in_specs,
        out_specs=[VMEM] * len(outs),
        out_shape=[jax.ShapeDtypeStruct(shape, jnp.bfloat16) for shape in outs],
        scratch_shapes=scratch,
        cost_estimate=pl.CostEstimate(flops=0, bytes_accessed=0, transcendentals=0),
        compiler_params=pltpu.CompilerParams(vmem_limit_bytes=limit * 2**20),
    )(*ins)


def attention(spots, base, rows, allowed, pieces, qkv_width):
    length, width = rows.shape
    heads = qkv_width // (3 * HEAD_DIM)
    half = length // 2
    qkv_end, out_start = -(-qkv_width // 128) * 128, qkv_width // 128 * 128

    masks = [] if allowed is None else [allowed]

    def kernel(spots_ref, rows_ref, *refs):
        if allowed is None:
            seen = lax.broadcasted_iota(jnp.int32, (length, length), 0) >= lax.broadcasted_iota(
                jnp.int32, (length, length), 1
            )
        else:
            seen = refs[0][...] > 0
            refs = refs[1:]
        piece_refs = refs[: len(pieces)]
        keep, send, weight, projected, mixed, sems = refs[len(pieces) :]
        copies = load_weight(spots_ref, base, piece_refs, weight, sems)
        normed = norm(rows_ref[...].astype(jnp.float32))
        mixed[...] = jnp.zeros_like(mixed)
        for copy in copies:
            copy.wait()
        projected[:, :qkv_end] = (
            jnp.dot(normed, weight[:, :qkv_end], preferred_element_type=jnp.float32)
            .astype(jnp.bfloat16)
            .astype(jnp.float32)
        )
        for head in range(heads):
            at = head * 3 * HEAD_DIM
            query = projected[:, at : at + HEAD_DIM].astype(jnp.bfloat16)
            key = projected[:, at + HEAD_DIM : at + 2 * HEAD_DIM].astype(jnp.bfloat16)
            value = projected[:, at + 2 * HEAD_DIM : at + 3 * HEAD_DIM].astype(jnp.bfloat16)
            scores = dot_t(query, key) * HEAD_DIM ** (-0.5)
            scores = jnp.where(seen, scores, -1e30)
            exponent = jnp.exp(scores - jnp.max(scores, axis=-1, keepdims=True))
            soft = (exponent / jnp.sum(exponent, axis=-1, keepdims=True)).astype(jnp.bfloat16)
            out_at = qkv_width + head * HEAD_DIM
            mixed[:, out_at : out_at + HEAD_DIM] = jnp.dot(
                soft, value, preferred_element_type=jnp.float32
            )
        projected[...] = dot_t(mixed[:, out_start:].astype(jnp.bfloat16), weight[:, out_start:])
        core = spots_ref[24]
        keep[...] = projected[pl.ds(pl.multiple_of(core * half, 16), half), :].astype(jnp.bfloat16)
        send[...] = projected[pl.ds(pl.multiple_of((1 - core) * half, 16), half), :].astype(
            jnp.bfloat16
        )

    return local_call(
        kernel,
        [spots, rows] + masks + pieces,
        [SMEM, VMEM] + [VMEM] * len(masks) + [ANY] * len(pieces),
        [(half, width)] * 2,
        [
            pltpu.VMEM((width, width), jnp.bfloat16),
            pltpu.VMEM((length, width), jnp.float32),
            pltpu.VMEM((length, width), jnp.float32),
            pltpu.SemaphoreType.DMA((8,)),
        ],
    )


def middle(spots, rows, left, right):
    half, width = left.shape

    def kernel(spots_ref, rows_ref, left_ref, right_ref, mid, normed):
        base = rows_ref[pl.ds(pl.multiple_of(spots_ref[24] * half, 16), half), :]
        total = left_ref[...].astype(jnp.float32) + right_ref[...].astype(jnp.float32)
        value = (base.astype(jnp.float32) + total).astype(jnp.bfloat16)
        mid[...] = value
        normed[...] = norm(value.astype(jnp.float32))

    return local_call(
        kernel, [spots, rows, left, right], [SMEM, VMEM, VMEM, VMEM], [(half, width)] * 2, [], 16
    )


def feed_forward(spots, sources, weights, bases):
    half, width = sources[0].shape
    units = width // 2
    pieces = [piece for weight in weights for piece in weight]
    parts = len(weights)
    rows = len(sources)

    def kernel(spots_ref, *refs):
        source_refs, piece_refs, refs = (
            refs[:rows],
            refs[rows : rows + len(pieces)],
            refs[rows + len(pieces) :],
        )
        targets, scratch = refs[:rows], refs[rows:]
        copies, at = [], 0
        for part in range(parts):
            mine = piece_refs[at : at + len(weights[part])]
            at += len(mine)
            copies += load_weight(spots_ref, bases[part], mine, scratch[part], scratch[parts + part])
        for copy in copies:
            copy.wait()
        if parts == 1:
            up, down = scratch[0][:, :units], scratch[0][:, units:]
        else:
            up, down = scratch[0][...], scratch[1][...]
        hidden = jnp.concatenate([source[...] for source in source_refs], axis=0)
        hidden = jnp.dot(hidden, up, preferred_element_type=jnp.float32)
        hidden = 0.5 * hidden * (1.0 + lax.erf(hidden * 0.5**0.5))
        result = dot_t(hidden.astype(jnp.bfloat16), down).astype(jnp.bfloat16)
        for at, target in enumerate(targets):
            target[...] = result[at * half : (at + 1) * half]

    return local_call(
        kernel,
        [spots] + sources + pieces,
        [SMEM] + [VMEM] * rows + [ANY] * len(pieces),
        [(half, width)] * rows,
        [pltpu.VMEM((width, weight[0].shape[1]), jnp.bfloat16) for weight in weights]
        + [pltpu.SemaphoreType.DMA((8,))] * parts,
    )


def merge(spots, base, blocks, pieces):
    count, width = blocks.shape
    half = width // 2

    def kernel(spots_ref, blocks_ref, *refs):
        piece_refs = refs[: len(pieces)]
        keep, send, weight, sems = refs[len(pieces) :]
        for copy in load_weight(spots_ref, base, piece_refs, weight, sems):
            copy.wait()
        core = spots_ref[24]
        source = blocks_ref[...]
        for side, target in ((core, keep), (1 - core, send)):
            rows = weight[pl.ds(pl.multiple_of(side * half, 16), half), :]
            target[...] = dot_t(source, rows).astype(jnp.bfloat16)

    return local_call(
        kernel,
        [spots, blocks] + pieces,
        [SMEM, VMEM] + [ANY] * len(pieces),
        [(count, half)] * 2,
        [pltpu.VMEM((width, width), jnp.bfloat16), pltpu.SemaphoreType.DMA((8,))],
    )


def pick(rows, which, axis):
    return lax.dynamic_index_in_dim(rows, which, axis, keepdims=False)


def add_short(left, right):
    return left.astype(jnp.float32) + right.astype(jnp.float32)


def join_core(half, axis):
    _, _, _, c = place()
    other = swap_core(half)
    first = jnp.where(c == 0, half, other)
    second = jnp.where(c == 0, other, half)
    return jnp.concatenate([first, second], axis=axis)


def exchange_y(blocks):
    _, y, _, _ = place()
    groups = blocks.shape[1]
    if groups > 1:
        members = [[i * groups + g for g in range(groups)] for i in range(8)]
        blocks = lax.all_to_all(
            blocks, "req", split_axis=1, concat_axis=1, tiled=True, axis_index_groups=members
        )
    blocks = blocks.reshape((4, 2) + blocks.shape[1:])
    return jnp.stack([pick(blocks, y, 1), swap_y(pick(blocks, 1 - y, 1))], axis=1)


def exchange_z(both):
    z, _, _, _ = place()
    mixed = [pick(both, z, 0)] + [swap_z(pick(both, z ^ k, 0), k) for k in (1, 2, 3)]
    return jnp.concatenate(mixed, axis=0)


def on_device(
    patches,
    half_grid,
    text_embed,
    dest_dev,
    dest_pos,
    text_len,
    enc_qkv,
    enc_out_t,
    enc_up,
    enc_down_t,
    merge_t,
    dec_qkv,
    dec_out_t,
    dec_up,
    dec_down_t,
):
    _, _, x, c = place()
    senders = lax.axis_size("req")
    image_count = half_grid.shape[0]
    model_width = patches.shape[1]
    cells = HALF * HALF
    slot_count = image_count * cells
    qkv_width = enc_qkv.shape[1]
    half_width = model_width // 2
    spots = block_places()

    enc_attn = own_rows(jnp.concatenate([enc_qkv, enc_out_t], axis=1))
    enc_up, enc_down_t = own_rows(enc_up), own_rows(enc_down_t)
    merge_t = own_rows(merge_t)
    dec_attn = own_rows(jnp.concatenate([dec_qkv, dec_out_t], axis=1))
    dec_up, dec_down_t = own_rows(dec_up), own_rows(dec_down_t)

    first, second, y_own = swap_z(enc_attn, 1), swap_z(enc_attn, 2), swap_y(enc_attn)
    first, second, y_own, enc_up, enc_down_t = together(first, second, y_own, enc_up, enc_down_t)
    third = swap_z(second, 1)
    y_early = swap_y(jnp.concatenate([first, second], axis=0))

    up, down = halves_by_z(enc_up), halves_by_z(enc_down_t)
    mine, others = [jnp.concatenate(pair, axis=1) for pair in zip(up, down)]
    third, near = together(third, others)
    enc_ff = Halved(mine, others, near)
    enc_attn = [enc_attn, first, second, third, y_own, y_early, swap_y(third)]
    enc_ff.third, merge_t = together(enc_ff.third, merge_t)
    enc_ff = enc_ff.pieces()

    merge_second = swap_z(merge_t, 2)

    cell_index = jnp.arange(cells, dtype=jnp.int32)
    slot_valid = ((cell_index // HALF)[None, :] < half_grid[:, 0:1]) & (
        (cell_index % HALF)[None, :] < half_grid[:, 1:2]
    )
    slot_valid = slot_valid.reshape(-1)

    rows = patches.reshape(image_count, HALF, 2, HALF, 2, model_width)
    rows = rows.transpose(4, 2, 0, 1, 3, 5).reshape(4 * slot_count, model_width)
    image_of = jnp.tile(jnp.arange(slot_count, dtype=jnp.int32) // cells, 4)
    allowed = (image_of[:, None] == image_of[None, :]) & jnp.tile(slot_valid, 4)[None, :]
    allowed = allowed.astype(jnp.float32)

    keep, send = attention(spots, DIRECT, rows, allowed, enc_attn, qkv_width)
    mine = add_short(keep, swap_core(send)).astype(jnp.bfloat16)
    mid, normed = middle(spots, rows, mine, swap_x(mine))
    normed_pair = swap_z(normed, 1)
    normed_pair, merge_second = together(normed_pair, merge_second)
    sources = [normed, swap_core(normed), normed_pair, swap_core(normed_pair)]
    merge_two = jnp.concatenate([merge_t, merge_second], axis=0)
    merge_pair = swap_z(merge_two, 1)
    merge_two_y = swap_y(merge_two)
    own_keep, own_send, pair_keep, pair_send = feed_forward(spots, sources, [enc_ff], [DIRECT])
    pair_sum = add_short(pair_keep, swap_core(pair_send)).astype(jnp.bfloat16)
    pair_sum, merge_pair, merge_two_y, dec_attn = together(
        pair_sum, merge_pair, merge_two_y, dec_attn
    )
    arrived = swap_z(pair_sum, 1)
    attn_second = swap_z(dec_attn, 2)
    merge_all = [merge_two, merge_two_y, merge_pair, swap_y(merge_pair)]
    own_sum = add_short(own_keep, swap_core(own_send))
    total = (own_sum + arrived.astype(jnp.float32)).astype(jnp.bfloat16)
    total = total.reshape(2, slot_count, model_width)
    total = add_short(pick(total, x, 0), swap_x(pick(total, 1 - x, 0)))
    kept = pick(mid.reshape(2, slot_count, model_width), x, 0)
    encoded = (kept.astype(jnp.float32) + total).astype(jnp.bfloat16)

    encoded, attn_second = together(encoded, attn_second)
    attn_two = jnp.concatenate([dec_attn, attn_second], axis=0)
    attn_pair = swap_z(attn_two, 1)
    attn_two_y = swap_y(attn_two)
    keep, send = merge(spots, WHOLE, encoded, merge_all)
    merged = add_short(keep, swap_core(send))
    merged = merged.astype(jnp.bfloat16)
    merged = add_short(merged, swap_x(merged)).astype(jnp.bfloat16)

    even_share = slot_count // senders
    capacity = even_share + max(even_share // 2, 1)
    padded = -(-capacity // 16) * 16
    one_hot = (dest_dev[:, None] == jnp.arange(senders, dtype=jnp.int32)[None, :]).astype(jnp.int32)
    earlier = jnp.cumsum(one_hot, axis=0) - one_hot
    slot_rank = jnp.sum(earlier * one_hot, axis=1)
    bucket = dest_dev * padded + slot_rank
    chosen = jnp.arange(senders * padded, dtype=jnp.int32)[:, None] == bucket[None, :]
    digits = jnp.stack([slot_valid.astype(jnp.int32), dest_pos // 128, dest_pos % 128], 1)
    digits = jnp.pad(digits, ((0, 0), (0, 125))).astype(jnp.bfloat16)
    outgoing = jnp.dot(
        chosen.astype(jnp.bfloat16),
        jnp.concatenate([merged, digits], axis=1),
        preferred_element_type=jnp.float32,
    ).astype(jnp.bfloat16)
    outgoing, attn_pair, attn_two_y, dec_up = together(outgoing, attn_pair, attn_two_y, dec_up)
    mine, others = halves_by_z(dec_up)
    dec_up = Halved(mine, others, others)
    both = exchange_y(outgoing.reshape(8, senders // 8, padded, -1))
    both, attn_pair = together(both, attn_pair)
    dec_up = dec_up.pieces()
    attn_pair_y = swap_y(attn_pair)
    incoming = exchange_z(both)
    incoming, attn_pair_y, dec_down_t = together(incoming, attn_pair_y, dec_down_t)
    dec_attn = [attn_two, attn_two_y, attn_pair, attn_pair_y]
    dec_down = halved_column(dec_down_t)
    incoming = incoming.reshape(senders * padded, -1)

    seq_len = text_embed.shape[0]
    half_rows = seq_len // 2
    positions = jnp.arange(seq_len, dtype=jnp.int32)
    marks = incoming[:, half_width:].astype(jnp.int32)
    target = jnp.where(marks[:, 0] > 0, marks[:, 1] * 128 + marks[:, 2], -1)
    hits = positions[:, None] == target[None, :]
    placed = jnp.dot(
        hits.astype(jnp.bfloat16), incoming[:, :half_width], preferred_element_type=jnp.float32
    ).astype(jnp.bfloat16)
    text_half = lax.dynamic_slice_in_dim(text_embed, c * half_width, half_width, 1)
    dec_half = jnp.where(jnp.any(hits, axis=1)[:, None], placed, text_half)
    rows = join_core(dec_half, 1)
    causal = None
    keep, send = attention(spots, WHOLE, rows, causal, dec_attn, qkv_width)
    send, *dec_up = together(send, *dec_up)
    mine = add_short(keep, swap_core(send)).astype(jnp.bfloat16)
    mid, normed = middle(spots, rows, mine, swap_x(mine))
    normed_pair = swap_z(normed, 1)
    sources = [normed, swap_core(normed), normed_pair, swap_core(normed_pair)]
    own_keep, own_send, pair_keep, pair_send = feed_forward(spots, sources, [dec_up, dec_down], [DIRECT, COLUMNS])
    pair_sum = add_short(pair_keep, swap_core(pair_send)).astype(jnp.bfloat16)
    arrived = swap_z(pair_sum, 1)
    own_sum = add_short(own_keep, swap_core(own_send))
    total = (own_sum + arrived.astype(jnp.float32)).astype(jnp.bfloat16)
    total = add_short(total, swap_x(total))
    decoded = (mid.astype(jnp.float32) + total).astype(jnp.bfloat16)
    keep_mask = positions < slot_count + text_len[0]
    keep_half = pick(keep_mask.reshape(2, half_rows), c, 0)
    decoded = jnp.where(keep_half[:, None], decoded, jnp.zeros_like(decoded))
    return join_core(decoded, 0)


def solution(mesh):
    return jax.shard_map(
        on_device,
        mesh=mesh,
        in_specs=(
            P("req", None),
            P("req", None),
            P("req", None),
            P("req"),
            P("req"),
            P("req"),
            P("req", "tp"),
            P("req", "tp"),
            P("req", "tp"),
            P("req", "tp"),
            P("req", "tp"),
            P("req", "tp"),
            P("req", "tp"),
            P("req", "tp"),
            P("req", "tp"),
        ),
        out_specs=P("req", None),
        check_vma=False,
    )
```
